32 devices in a mesh: mlong: 8 (over y, x, core), mshort: 4 (over z).
Axes of the slice: x: 2, y: 2, z: 4, core: 2. Of those that a mesh axis runs over, the one named last changes fastest.
Arguments:
- acq_traces: bfloat16 [16384, 1024], P(('mlong', 'mshort')), may hold values from -6 to 6
- route_owner: int32 [16384], P(('mlong', 'mshort')), may hold values from -1 to 31, as said below
- route_row: int32 [16384], P(('mlong', 'mshort')), may hold values from -1 to 511, as said below
- route_fold: int32 [16384], P(('mlong', 'mshort')), may hold values from 0 to 3
- sample_bits: int32 [16384, 64], P(('mlong', 'mshort')), may hold values from 0 to 65535
- left_factors: bfloat16 [16384, 4, 128], P(('mlong', 'mshort')), may hold values from -0.5 to 0.5
- right_factors: bfloat16 [4, 32768, 128], P(None, ('mlong', 'mshort')), may hold values from -6 to 6
Outputs:
- new_right: float32 [4, 32768, 128], P(None, ('mlong', 'mshort'))
- trace_residuals: bfloat16 [16384, 1024], P(('mlong', 'mshort'))
The draws below stay inside these ranges and needn't reach their ends.
Inputs may be any that keep to these rules, and one draw needn't show every extreme that they name: route_owner: -1 marks an empty slot. In each device's 16 * 32 slots no owner is named more than 16 times; some owner is named exactly 16 times in every device's slots. Every owner is named somewhere. route_row: -1 exactly where route_owner is -1. No pair (route_owner, route_row) occurs twice.
All inputs are finite; a program needn't handle non-finite values.
Results may differ from the reference program's by a relative error of at most 0.0036.
Values may be sent and summed in bfloat16 or wider, within the bound.
A program may use at most 64 MiB of HBM per device.

```python
import jax
import jax.numpy as jnp
from jax import lax

W = 1024
RANK = 128
FOLDS = 4
H = 4
CX = 16
CY = 32
NX = 128
NY = 128
NROWS = 16384
NCOLS = 32768
N_MLONG = 8
N_MSHORT = 4


def routing(key):
    rows = CX * CY
    peers = NROWS // rows
    cap = rows // peers
    keys = jax.random.split(key, 5)
    full_dest = jax.random.randint(keys[0], (), 0, peers)
    hot = jax.random.randint(keys[1], (peers,), 1, 2 * cap + 1)
    raw = jax.random.randint(keys[2], (peers, peers), 0, 2 * cap + 1)
    count = jnp.minimum(jnp.minimum(raw, hot[None, :]), cap - 1)
    count = jnp.maximum(count, jnp.eye(peers, dtype=jnp.int32))
    dest = jnp.arange(peers, dtype=jnp.int32)
    count = jnp.where(dest[None, :] == full_dest, cap, count)
    offset = jnp.cumsum(count, axis=0) - count
    perms = jax.vmap(lambda k: jax.random.permutation(k, rows))(jax.random.split(keys[3], peers)).astype(jnp.int32)
    slot = jnp.arange(cap, dtype=jnp.int32)
    live = slot[None, None, :] < count[:, :, None]
    index = jnp.minimum(offset[:, :, None] + slot[None, None, :], rows - 1)
    chosen = perms[jnp.broadcast_to(dest[None, :, None], index.shape), index]
    owner = jnp.where(live, jnp.broadcast_to(dest[None, :, None], index.shape), -1).reshape(peers, rows)
    local = jnp.where(live, chosen, -1).reshape(peers, rows)
    order = jax.vmap(lambda k: jax.random.permutation(k, rows))(jax.random.split(keys[4], peers)).astype(jnp.int32)
    owner = jnp.take_along_axis(owner, order, axis=1)
    local = jnp.take_along_axis(local, order, axis=1)
    return (owner.reshape(-1).astype(jnp.int32), local.reshape(-1).astype(jnp.int32))


def draw_route_owner(key, part):
    return routing(key)[0]


def draw_route_row(key, part):
    return routing(key)[1]


def plant(values, key, low, largest):
    longest = values.shape.index(max(values.shape))
    spots = []
    for shift in (0, 1):
        where = [jax.random.randint(jax.random.fold_in(key, axis), (), 0, length) for axis, length in enumerate(values.shape)]
        where[longest] = (where[longest] + shift) % values.shape[longest]
        spots.append(tuple(where))
    return values.at[spots[0]].set(low).at[spots[1]].set(largest)


def block_levels(stream_key, extent, pieces, least, high):
    factor_of = 1.0
    for axis_at, shards_of in pieces:
        heights = jax.random.uniform(jax.random.fold_in(jax.random.fold_in(stream_key, 6), axis_at), (shards_of,), jnp.float32, least / len(pieces), high / len(pieces))
        factor_of = factor_of * jnp.repeat(jnp.exp(heights), extent[axis_at] // shards_of).reshape((-1,) + (1,) * (len(extent) - 1 - axis_at))
    return factor_of


def normal_values(rng, shape, width, bound, cuts=(), kind=jnp.bfloat16):
    factor_of = block_levels(rng, shape, cuts, -0.22, 0.18) if cuts else 1.0
    values = jax.random.normal(rng, shape, jnp.float32) * width * factor_of
    return jnp.minimum(jnp.maximum(values, -bound), bound).astype(kind)


def setup_inputs(seed: int = 0) -> dict:
    key_list = jax.random.split(jax.random.key(seed), 8)
    acq_traces = normal_values(key_list[0], (NROWS, W), 1.0, 6.0, ((0, 32),))
    route_owner = draw_route_owner(jax.random.fold_in(key_list[7], 71), 0)
    route_row = draw_route_row(jax.random.fold_in(key_list[7], 71), 0)
    route_fold = plant(jax.random.randint(key_list[3], (NROWS,), 0, FOLDS), jax.random.fold_in(key_list[3], 1), 0, FOLDS - 1).astype(jnp.int32)
    sample_bits = plant(jax.random.randint(key_list[4], (NROWS, W // 16), 0, 65536), jax.random.fold_in(key_list[4], 1), 0, 65535).astype(jnp.int32)
    left_factors = normal_values(key_list[5], (NROWS, FOLDS, RANK), RANK ** -0.5, 0.5, ((0, 32),))
    right_factors = normal_values(key_list[6], (FOLDS, NCOLS, RANK), 1.0, 6.0, ((1, 32),))
    return {"acq_traces": acq_traces, "route_owner": route_owner, "route_row": route_row, "route_fold": route_fold, "sample_bits": sample_bits, "left_factors": left_factors, "right_factors": right_factors}


def unpack(bits):
    shifts = jnp.arange(16, dtype=jnp.int32)
    flags = jnp.bitwise_and(lax.shift_right_logical(bits[:, :, None], shifts[None, None, :]), 1)
    return flags.reshape(bits.shape[0], -1).astype(jnp.float32)

def chol_right(cross, gram):
    chol = jnp.linalg.cholesky(gram)
    first = lax.linalg.triangular_solve(chol, cross, left_side=False, lower=True, transpose_a=True)
    return lax.linalg.triangular_solve(chol, first, left_side=False, lower=True, transpose_a=False)

def to_grid(values):
    tail = values.shape[1:]
    values = values.reshape((N_MLONG, N_MSHORT, CX, CY) + tail)
    values = jnp.moveaxis(values, 2, 1)
    return values.reshape((NX, NY) + tail)

def reference(acq_traces, route_owner, route_row, route_fold, sample_bits, left_factors, right_factors):
    rows = CX * CY
    peers = N_MLONG * N_MSHORT
    valid = route_owner >= 0
    target = jnp.where(valid, route_owner * rows + route_row, NROWS).astype(jnp.int32)
    data = jnp.zeros((NROWS, W), jnp.bfloat16).at[target].set(acq_traces, mode='drop')
    fold = jnp.full((NROWS,), -1, jnp.int32).at[target].set(route_fold, mode='drop')
    pad2 = ((H, H), (H, H))
    data_p = jnp.pad(to_grid(data), pad2 + ((0, 0),))
    bits_p = jnp.pad(to_grid(sample_bits), pad2 + ((0, 0),))
    fold_p = jnp.pad(to_grid(fold), pad2, constant_values=-1)
    left_p = jnp.pad(to_grid(left_factors), pad2 + ((0, 0), (0, 0)))
    ridge = jnp.eye(RANK, dtype=jnp.float32)
    wx = CX + 2 * H
    wy = CY + 2 * H

    def window(dev):
        xa = dev // N_MSHORT * CX
        yb = dev % N_MSHORT * CY
        zero = jnp.zeros((), jnp.int32)
        d_win = lax.dynamic_slice(data_p, (xa, yb, zero), (wx, wy, W))
        b_win = lax.dynamic_slice(bits_p, (xa, yb, zero), (wx, wy, W // 16))
        f_win = lax.dynamic_slice(fold_p, (xa, yb), (wx, wy))
        l_win = lax.dynamic_slice(left_p, (xa, yb, zero, zero), (wx, wy, FOLDS, RANK))
        v_win = lax.dynamic_slice(right_factors, (zero, dev * W, zero), (FOLDS, W, RANK))
        d_core = d_win[H:H + CX, H:H + CY].reshape(rows, W)
        f_core = f_win[H:H + CX, H:H + CY].reshape(rows)
        l_core = l_win[H:H + CX, H:H + CY].reshape(rows, FOLDS, RANK)
        s_core = unpack(b_win[H:H + CX, H:H + CY].reshape(rows, W // 16)) * (f_core >= 0)[:, None].astype(jnp.float32)
        d_win = d_win.reshape(-1, W)
        f_win = f_win.reshape(-1)
        l_win = l_win.reshape(-1, FOLDS, RANK)
        seen = unpack(b_win.reshape(-1, W // 16)) * (f_win >= 0)[:, None].astype(jnp.float32)
        news = []
        chosen = jnp.zeros((rows, W), jnp.float32)
        for f in range(FOLDS):
            lf = l_win[:, f]
            pred = jnp.dot(lf.astype(jnp.float32), v_win[f].T.astype(jnp.float32), preferred_element_type=jnp.float32)
            train = seen * (f_win != f)[:, None].astype(jnp.float32)
            filled = (train * d_win.astype(jnp.float32) + (1.0 - train) * pred).astype(jnp.bfloat16)
            cross = jnp.dot(filled.T.astype(jnp.float32), lf.astype(jnp.float32), preferred_element_type=jnp.float32)
            gram = jnp.dot(lf.T.astype(jnp.float32), lf.astype(jnp.float32), preferred_element_type=jnp.float32) + ridge
            newv = chol_right(cross, gram)
            news.append(newv)
            core_pred = jnp.dot(l_core[:, f].astype(jnp.float32), newv.astype(jnp.bfloat16).T.astype(jnp.float32), preferred_element_type=jnp.float32)
            chosen = chosen + (f_core == f)[:, None].astype(jnp.float32) * core_pred
        resid = (s_core * (d_core.astype(jnp.float32) - chosen)).astype(jnp.bfloat16)
        return (jnp.stack(news), resid)
    news, resid = lax.map(window, jnp.arange(peers, dtype=jnp.int32))
    new_right = jnp.moveaxis(news, 0, 1).reshape(FOLDS, NCOLS, RANK)
    resid = resid.reshape(NROWS, W)
    picked = jnp.take(resid, jnp.minimum(target, NROWS - 1), axis=0)
    trace_residuals = jnp.where(valid[:, None], picked, jnp.zeros((), jnp.bfloat16))
    return (new_right, trace_residuals)
```

```python
import functools

import jax
import jax.numpy as jnp
from jax import lax
from jax.experimental import pallas as pl
from jax.experimental.pallas import tpu as pltpu
from jax.sharding import PartitionSpec as P

RANK = 128
FOLDS = 4
H = 4
CX = 16
CY = 32


def padded(x, sides, width):
    for axis, dim in sides:
        count, length = (lax.axis_size(axis), x.shape[dim])
        up = [(i, (i + 1) % count) for i in range(count - 1)]
        down = [(j, i) for i, j in up]
        last = lax.slice_in_dim(x, length - width, length, axis=dim)
        initial = lax.slice_in_dim(x, 0, width, axis=dim)
        before = lax.ppermute(last, axis, up)
        after = lax.ppermute(initial, axis, down)
        x = jnp.concatenate([before, x, after], axis=dim)
    return x


def unpack(bits):
    shifts = jnp.arange(16, dtype=jnp.int32)
    flags = jnp.bitwise_and(lax.shift_right_logical(bits[:, :, None], shifts[None, None, :]), 1)
    return flags.reshape(bits.shape[0], -1).astype(jnp.float32)


def chol_right(cross, gram):
    chol = jnp.linalg.cholesky(gram)
    first = lax.linalg.triangular_solve(chol, cross, left_side=False, lower=True, transpose_a=True)
    return lax.linalg.triangular_solve(chol, first, left_side=False, lower=True, transpose_a=False)


def local(acq_traces, route_owner, route_row, route_fold, sample_bits, left_factors, right_factors):
    n_long = lax.axis_size("mlong")
    n_short = lax.axis_size("mshort")
    peers = n_long * n_short
    rows = acq_traces.shape[0]
    width = acq_traces.shape[1]
    cap = rows // peers
    total = peers * cap
    grid_bits = sample_bits.reshape(CX, CY, width // 16)
    grid_left = left_factors.reshape(CX, CY, FOLDS * RANK)
    valid = route_owner >= 0
    owner = jnp.where(valid, route_owner, 0)
    onehot = (
        (owner[:, None] == jnp.arange(peers, dtype=jnp.int32)[None, :]) & valid[:, None]
    ).astype(jnp.int32)
    within = jnp.sum(jnp.cumsum(onehot, axis=0) * onehot, axis=1) - 1
    place = jnp.where(valid, owner * cap + within, total)
    source = (
        jnp.full((total,), rows, jnp.int32)
        .at[place]
        .set(jnp.arange(rows, dtype=jnp.int32), mode="drop")
    )
    filled_slot = source < rows
    pick = jnp.minimum(source, rows - 1)
    send_traces = jnp.where(
        filled_slot[:, None], jnp.take(acq_traces, pick, axis=0), jnp.zeros((), jnp.bfloat16)
    )
    send_rows = jnp.where(filled_slot, jnp.take(route_row, pick), -1)
    send_folds = jnp.where(filled_slot, jnp.take(route_fold, pick), -1)
    got_traces, got_rows, got_folds = (
        lax.all_to_all(send_traces, ("mlong", "mshort"), split_axis=0, concat_axis=0, tiled=True),
        lax.all_to_all(send_rows, ("mlong", "mshort"), split_axis=0, concat_axis=0, tiled=True),
        lax.all_to_all(send_folds, ("mlong", "mshort"), split_axis=0, concat_axis=0, tiled=True),
    )
    arrival = (
        jnp.full((rows,), total, jnp.int32)
        .at[jnp.where(got_rows >= 0, got_rows, rows)]
        .set(jnp.arange(total, dtype=jnp.int32), mode="drop")
    )
    present = arrival < total
    slot_at = jnp.minimum(arrival, total - 1)
    data = jnp.where(
        present[:, None], jnp.take(got_traces, slot_at, axis=0), jnp.zeros((), jnp.bfloat16)
    )
    fold = jnp.where(present, jnp.take(got_folds, slot_at), -1)
    wide_data, wide_bits, wide_fold, wide_left = (
        padded(data.reshape(CX, CY, width), (("mlong", 0), ("mshort", 1)), H),
        padded(grid_bits, (("mlong", 0), ("mshort", 1)), H),
        padded(fold.reshape(CX, CY), (("mlong", 0), ("mshort", 1)), H),
        padded(grid_left, (("mlong", 0), ("mshort", 1)), H),
    )
    d_win = wide_data.reshape(-1, width)
    f_win = wide_fold.reshape(-1)
    l_win = wide_left.reshape(-1, FOLDS, RANK)
    seen = unpack(wide_bits.reshape(-1, width // 16)) * (f_win >= 0)[:, None].astype(jnp.float32)
    s_core = unpack(sample_bits) * (fold >= 0)[:, None].astype(jnp.float32)
    ridge = jnp.eye(RANK, dtype=jnp.float32)
    updates = []
    chosen = jnp.zeros((rows, width), jnp.float32)
    for f in range(FOLDS):
        factor = l_win[:, f]
        pred = jnp.dot(factor, right_factors[f].T, preferred_element_type=jnp.float32)
        train = seen * (f_win != f)[:, None].astype(jnp.float32)
        imputed = (train * d_win.astype(jnp.float32) + (1.0 - train) * pred).astype(jnp.bfloat16)
        cross = jnp.dot(imputed.T, factor, preferred_element_type=jnp.float32)
        gram = jnp.dot(factor.T, factor, preferred_element_type=jnp.float32) + ridge
        update = chol_right(cross, gram)
        updates.append(update)
        core_pred = jnp.dot(
            left_factors[:, f], update.astype(jnp.bfloat16).T, preferred_element_type=jnp.float32
        )
        chosen = chosen + (fold == f)[:, None].astype(jnp.float32) * core_pred
    new_right = jnp.stack(updates)
    resid = (s_core * (data.astype(jnp.float32) - chosen)).astype(jnp.bfloat16)
    back = jnp.where(
        (got_rows >= 0)[:, None],
        jnp.take(resid, jnp.maximum(got_rows, 0), axis=0),
        jnp.zeros((), jnp.bfloat16),
    )
    returned = lax.all_to_all(back, ("mlong", "mshort"), split_axis=0, concat_axis=0, tiled=True)
    trace_residuals = jnp.where(
        valid[:, None],
        jnp.take(returned, jnp.minimum(place, total - 1), axis=0),
        jnp.zeros((), jnp.bfloat16),
    )
    return (new_right, trace_residuals)


MESH = pl.DeviceIdType.MESH
WIN = 1024
CORE = CX * CY
WIDE = FOLDS * RANK
NT = (((1,), (1,)), ((), ()))
HALO = (
    (1, 0, False, CORE - H * CY, CORE, H * CY),
    (-1, 0, False, 0, CORE + H * CY, H * CY),
    (0, 1, True, H * CX, CORE + 2 * H * CY, H * CX),
    (0, -1, True, 0, CORE + 2 * H * CY + H * CX, H * CX),
    (1, 1, True, 2 * H * CX + 48, CORE + 2 * H * (CX + CY), 16),
    (1, -1, True, 2 * H * CX + 32, CORE + 2 * H * (CX + CY) + 16, 16),
    (-1, 1, True, 2 * H * CX + 16, CORE + 2 * H * (CX + CY) + 32, 16),
    (-1, -1, True, 2 * H * CX, CORE + 2 * H * (CX + CY) + 48, 16),
)
PACK = 2 * H * CX + 64


def iota(shape, dim):
    return lax.broadcasted_iota(jnp.int32, shape, dim)


def flags(mask, dtype=jnp.bfloat16):
    return jnp.where(mask, 1.0, 0.0).astype(dtype)


def dot(a, b, dims=(((1,), (0,)), ((), ())), precision=None):
    return lax.dot_general(a, b, dims, precision=precision, preferred_element_type=jnp.float32)


def packed_rows(shape):
    t = iota(shape, 0)
    u = t - 2 * H * CX
    side = jnp.where(t < H * CX, 0, CY - H)
    v = jnp.where(t < H * CX, t, t - H * CX)
    edge = (v // H) * CY + v % H + side
    k = u // 16
    w = u % 16
    corner = (w // H + jnp.where(k >= 2, CX - H, 0)) * CY + w % H + jnp.where(k % 2 == 1, CY - H, 0)
    return jnp.where(u < 0, edge, corner)


def kernel(
    n_long, n_short, traces, own, row, fold, side, right, news, out,
    lw, lpack, dw, dpack, meta_out, meta_in, send, got, ret, back, pred, seen, cross, lt, gram, vmat, qmat, resid, newb,
    meta_s, meta_r, data_s, data_r, ret_s, ret_r, hl_s, hl_r, hd_s, hd_r,
):
    peers = n_long * n_short
    cap = CORE // peers
    a = lax.axis_index("mlong")
    c = lax.axis_index("mshort")
    me = a * n_short + c
    width = traces.shape[1]

    lw[0:CORE, :] = side[...]
    lw[CORE:WIN, :] = jnp.zeros((WIN - CORE, WIDE + 128), jnp.bfloat16)
    dw[CORE:WIN, width : width + 128] = jnp.zeros((WIN - CORE, 128), jnp.bfloat16)

    barrier = pltpu.get_barrier_semaphore()

    def greet(k, carry):
        q = lax.rem(me + k, peers)
        pl.semaphore_signal(barrier, inc=1, device_id=(q // n_short, lax.rem(q, n_short)), device_id_type=MESH)
        return carry

    lax.fori_loop(1, peers, greet, 0)

    pick = flags(packed_rows((PACK, CORE)) == iota((PACK, CORE), 1))
    lpack[...] = dot(pick, side[...]).astype(jnp.bfloat16)

    owner = own[...]
    oh = flags(iota((peers, CORE), 0) == owner, jnp.float32)
    tri = flags(iota((CORE, CORE), 0) < iota((CORE, CORE), 1))
    cum = dot(oh.astype(jnp.bfloat16), tri)
    within = jnp.sum(oh * cum, axis=0, keepdims=True).astype(jnp.int32)
    place = jnp.where(owner >= 0, owner * cap + within, -1)
    rows = row[...]
    vals = [(rows // 128).astype(jnp.float32), (rows % 128).astype(jnp.float32), (fold[...] + 1).astype(jnp.float32)]
    left = jnp.concatenate([oh * v for v in vals], axis=1).astype(jnp.bfloat16)
    rightm = jnp.concatenate([flags(iota((128, CORE), 0) == within + 32 * i) for i in range(3)], axis=1)
    meta = dot(left, rightm, NT)
    for p in range(peers):
        meta_out[p] = meta[p : p + 1, :]
    meta_in[me] = meta_out[me]

    pl.semaphore_wait(barrier, peers - 1)

    def halo(buffer, pack, send_sem, recv_sem, i):
        da, dc, packed, start, dst, count = HALO[i]
        here = pack if packed else buffer
        return pltpu.make_async_remote_copy(
            src_ref=here.at[pl.ds(start, count)],
            dst_ref=buffer.at[pl.ds(dst, count)],
            send_sem=send_sem.at[i],
            recv_sem=recv_sem.at[i],
            device_id=(a + da, c + dc),
            device_id_type=MESH,
        )

    def inside(da, dc):
        return (a + da >= 0) & (a + da < n_long) & (c + dc >= 0) & (c + dc < n_short)

    def halo_start(*refs):
        for i in range(8):
            @pl.when(inside(HALO[i][0], HALO[i][1]))
            def _():
                halo(*refs, i).start()

    def halo_recv(*refs):
        for i in range(8):
            @pl.when(inside(-HALO[i][0], -HALO[i][1]))
            def _():
                halo(*refs, i).wait_recv()

    def halo_sent(*refs):
        for i in range(8):
            @pl.when(inside(HALO[i][0], HALO[i][1]))
            def _():
                halo(*refs, i).wait_send()

    def swap(src, dst, send_sem, recv_sem, k):
        to = lax.rem(me + k, peers)
        return pltpu.make_async_remote_copy(
            src_ref=src.at[to],
            dst_ref=dst.at[me],
            send_sem=send_sem.at[k],
            recv_sem=recv_sem.at[k],
            device_id=(to // n_short, lax.rem(to, n_short)),
            device_id_type=MESH,
        )

    def arriving(src, dst, send_sem, recv_sem, k):
        origin = lax.rem(me + peers - k, peers)
        return pltpu.make_async_remote_copy(
            src_ref=src.at[origin],
            dst_ref=dst.at[origin],
            send_sem=send_sem.at[k],
            recv_sem=recv_sem.at[k],
            device_id=(origin // n_short, lax.rem(origin, n_short)),
            device_id_type=MESH,
        )

    def swap_start(*refs):
        def go(k, carry):
            swap(*refs, k).start()
            return carry

        lax.fori_loop(1, peers, go, 0)

    def swap_recv(*refs):
        def go(k, carry):
            arriving(*refs, k).wait_recv()
            return carry

        lax.fori_loop(1, peers, go, 0)

    def swap_sent(*refs):
        def go(k, carry):
            swap(*refs, k).wait_send()
            return carry

        lax.fori_loop(1, peers, go, 0)

    metas = (meta_out, meta_in, meta_s, meta_r)
    datas = (send, got, data_s, data_r)
    rets = (back, ret, ret_s, ret_r)
    lefts = (lw, lpack, hl_s, hl_r)
    halos = (dw, dpack, hd_s, hd_r)
    halo_start(*lefts)
    swap_start(*metas)

    def spread(t, carry):
        take = flags(iota((128, CORE), 0) + t * 128 == place)
        block = dot(take, traces[...]).astype(jnp.bfloat16)
        send[pl.ds(t * (128 // cap), 128 // cap)] = block.reshape(128 // cap, cap, width)
        return carry

    lax.fori_loop(0, CORE // 128, spread, 0)
    got[me] = send[me]
    swap_start(*datas)

    eye = iota((CORE, CORE), 0) == iota((CORE, CORE), 1)

    def column(line):
        return jnp.sum(jnp.where(eye, line.astype(jnp.float32), 0.0), axis=1, keepdims=True).astype(jnp.int32)

    qmat[...] = flags(column(place) == iota((CORE, CORE), 1))

    halo_recv(*lefts)
    for f in range(FOLDS):
        factor = lw[:, f * RANK : (f + 1) * RANK]
        lt[f] = factor.T
        ident = flags(iota((RANK, RANK), 0) == iota((RANK, RANK), 1), jnp.float32)
        gram[f] = dot(lt[f], factor) + ident

    def eliminate(b, carry):
        k0 = pl.multiple_of(b * 8, 8)
        panel = gram[:, pl.ds(k0, 8), :]
        first = panel
        lane = iota((FOLDS, 8, RANK), 2)
        sub = iota((FOLDS, 8, RANK), 1)
        for j in range(8):
            col = jnp.sum(jnp.where(lane == k0 + j, panel, 0.0), axis=2, keepdims=True)
            inv = 1.0 / col[:, j : j + 1, :]
            w = jnp.where(lane[:, 0:1, :] == k0 + j, inv, panel[:, j : j + 1, :] * inv)
            panel = jnp.where(sub == j, w, jnp.where(lane == k0 + j, 0.0, panel) - col * w)
        signed = jnp.where(lane < k0, -first, first)
        cols = iota((RANK, RANK), 1)
        for f in range(FOLDS):
            change = dot(signed[f].T, panel[f], precision=lax.Precision.HIGHEST)
            gram[f] = jnp.where((cols >= k0) & (cols < k0 + 8), 0.0, gram[f]) - change
        gram[:, pl.ds(k0, 8), :] = panel
        return carry

    lax.fori_loop(0, RANK // 8, eliminate, 0)

    words = iota((128, width), 0)
    offs = iota((128, width), 1)
    expand = flags(words == offs // 16 + jnp.where(offs % 16 >= 8, 64, 0))

    def masks(t, carry):
        r = pl.ds(pl.multiple_of(t * 128, 128), 128)
        byte = dot(lw[r, WIDE : WIDE + 128], expand).astype(jnp.int32)
        bit = lax.shift_right_logical(byte, iota((128, width), 1) % 8) & 1
        seen[r, :] = bit.astype(jnp.float32).astype(jnp.bfloat16)
        return carry

    lax.fori_loop(0, WIN // 128, masks, 0)

    for f in range(FOLDS):
        def predict(t, carry, f=f):
            r = pl.ds(pl.multiple_of(t * 128, 128), 128)
            pred[f, r, :] = dot(lw[r, f * RANK : (f + 1) * RANK], right[f], NT).astype(jnp.bfloat16)
            return carry

        lax.fori_loop(0, WIN // 128, predict, 0)

    swap_recv(*metas)
    meta_got = meta_in[:, 0, :].astype(jnp.bfloat16)
    mine = iota((peers, CORE), 0) == iota((peers, CORE), 1) // cap
    lines = []
    for i in range(3):
        place_of = flags(iota((128, CORE), 0) == iota((128, CORE), 1) % cap + 32 * i)
        lines.append(jnp.sum(jnp.where(mine, dot(meta_got, place_of), 0.0), axis=0, keepdims=True))
    got_row = jnp.where(lines[2] > 0.5, lines[0] * 128.0 + lines[1], -1.0).astype(jnp.int32)
    got_fold = jnp.broadcast_to(lines[2], (128, CORE)).astype(jnp.bfloat16)
    vmat[...] = flags(column(got_row) == iota((CORE, CORE), 1))

    swap_recv(*datas)
    arrived = got[...].reshape(CORE, width)

    take = flags(packed_rows((PACK, CORE)) == got_row)
    dpack[:, 0:width] = dot(take, arrived).astype(jnp.bfloat16)
    dpack[:, width : width + 128] = dot(take, got_fold, NT).astype(jnp.bfloat16)

    def gather(t, carry):
        r = pl.ds(pl.multiple_of(t * 128, 128), 128)
        take = flags(iota((128, CORE), 0) + t * 128 == got_row)
        dw[r, 0:width] = dot(take, got[...].reshape(CORE, width)).astype(jnp.bfloat16)
        dw[r, width : width + 128] = dot(take, got_fold, NT).astype(jnp.bfloat16)
        return carry

    lax.fori_loop(0, CORE // 128, gather, 0)
    halo_start(*halos)

    cross[...] = jnp.zeros_like(cross)

    def accumulate(t):
        r = pl.ds(t * 256, 256)
        kind = jnp.concatenate([dw[r, width : width + 128]] * (width // 128), axis=1) * seen[r, :]
        values = dw[r, 0:width]
        for f in range(FOLDS):
            train = (kind > 0.5) & (kind != f + 1.0)
            filled = jnp.where(train, values, pred[f, r, :])
            cross[f] += dot(lt[f, :, t * 256 : (t + 1) * 256], filled)

    accumulate(0)
    accumulate(1)
    halo_recv(*halos)
    accumulate(2)
    accumulate(3)

    for f in range(FOLDS):
        update = dot(gram[f], cross[f], precision=lax.Precision.HIGHEST)
        cross[f] = update
        newb[f * RANK : (f + 1) * RANK, :] = update.astype(jnp.bfloat16)

    def residual(t, carry):
        r = pl.ds(pl.multiple_of(t * 128, 128), 128)
        kind = dw[r, width : width + 128]
        zero = jnp.zeros((128, RANK), jnp.bfloat16)
        chosen_left = jnp.concatenate(
            [jnp.where(kind == f + 1.0, lw[r, f * RANK : (f + 1) * RANK], zero) for f in range(FOLDS)], axis=1
        )
        chosen = dot(chosen_left, newb[...])
        live = jnp.concatenate([kind] * (width // 128), axis=1) * seen[r, :]
        diff = dw[r, 0:width].astype(jnp.float32) - chosen
        resid[r, :] = jnp.where(live.astype(jnp.float32) > 0.5, diff, 0.0).astype(jnp.bfloat16)
        return carry

    lax.fori_loop(0, CORE // 128, residual, 0)

    def send_back(t, carry):
        r = pl.ds(pl.multiple_of(t * 128, 128), 128)
        block = dot(vmat[r, :], resid[...]).astype(jnp.bfloat16)
        back[pl.ds(t * (128 // cap), 128 // cap)] = block.reshape(128 // cap, cap, width)
        return carry

    lax.fori_loop(0, CORE // 128, send_back, 0)
    ret[me] = back[me]
    swap_start(*rets)

    for f in range(FOLDS):
        news[f] = cross[f].T

    swap_recv(*rets)

    def deliver(t, carry):
        r = pl.ds(pl.multiple_of(t * 128, 128), 128)
        out[r, :] = dot(qmat[r, :], ret[...].reshape(CORE, width)).astype(jnp.bfloat16)
        return carry

    lax.fori_loop(0, CORE // 128, deliver, 0)

    swap_sent(*metas)
    swap_sent(*datas)
    swap_sent(*rets)
    halo_sent(*lefts)
    halo_sent(*halos)


def fused(acq_traces, route_owner, route_row, route_fold, sample_bits, left_factors, right_factors):
    n_long = lax.axis_size("mlong")
    n_short = lax.axis_size("mshort")
    peers = n_long * n_short
    rows, width = acq_traces.shape
    cap = rows // peers
    low = jnp.bitwise_and(sample_bits, 255).astype(jnp.bfloat16)
    high = lax.shift_right_logical(sample_bits, 8).astype(jnp.bfloat16)
    side = jnp.concatenate([left_factors.reshape(rows, WIDE), low, high], axis=1)
    vmem = pl.BlockSpec(memory_space=pltpu.VMEM)
    bf = jnp.bfloat16
    dma = pltpu.SemaphoreType.DMA
    return pl.pallas_call(
        functools.partial(kernel, n_long, n_short),
        out_shape=(
            jax.ShapeDtypeStruct((FOLDS, width, RANK), jnp.float32),
            jax.ShapeDtypeStruct((rows, width), bf),
        ),
        in_specs=[vmem] * 6,
        out_specs=(vmem, vmem),
        scratch_shapes=[
            pltpu.VMEM((WIN, WIDE + 128), bf),
            pltpu.VMEM((PACK, WIDE + 128), bf),
            pltpu.VMEM((WIN, width + 128), bf),
            pltpu.VMEM((PACK, width + 128), bf),
            pltpu.VMEM((peers, 1, 128), jnp.float32),
            pltpu.VMEM((peers, 1, 128), jnp.float32),
            pltpu.VMEM((peers, cap, width), bf),
            pltpu.VMEM((peers, cap, width), bf),
            pltpu.VMEM((peers, cap, width), bf),
            pltpu.VMEM((peers, cap, width), bf),
            pltpu.VMEM((FOLDS, WIN, width), bf),
            pltpu.VMEM((WIN, width), bf),
            pltpu.VMEM((FOLDS, RANK, width), jnp.float32),
            pltpu.VMEM((FOLDS, RANK, WIN), bf),
            pltpu.VMEM((FOLDS, RANK, RANK), jnp.float32),
            pltpu.VMEM((CORE, CORE), bf),
            pltpu.VMEM((CORE, CORE), bf),
            pltpu.VMEM((CORE, width), bf),
            pltpu.VMEM((WIDE, width), bf),
            dma((peers,)), dma((peers,)), dma((peers,)), dma((peers,)), dma((peers,)), dma((peers,)),
            dma((8,)), dma((8,)), dma((8,)), dma((8,)),
        ],
        compiler_params=pltpu.CompilerParams(
            collective_id=0, has_side_effects=True, vmem_limit_bytes=56 * 1024 * 1024
        ),
    )(
        acq_traces, route_owner.reshape(1, rows), route_row.reshape(1, rows), route_fold.reshape(1, rows),
        side, right_factors,
    )


def solution(mesh):
    in_specs = (
        P(("mlong", "mshort"), None),
        P(("mlong", "mshort")),
        P(("mlong", "mshort")),
        P(("mlong", "mshort")),
        P(("mlong", "mshort"), None),
        P(("mlong", "mshort"), None, None),
        P(None, ("mlong", "mshort"), None),
    )
    out_specs = (P(None, ("mlong", "mshort"), None), P(("mlong", "mshort"), None))
    peers = mesh.shape["mlong"] * mesh.shape["mshort"]
    body = fused if peers * 16 == CX * CY else local
    return jax.shard_map(body, mesh=mesh, in_specs=in_specs, out_specs=out_specs, check_vma=False)
```

```python
import functools

import jax
import jax.numpy as jnp
from jax import lax
from jax.experimental import pallas as pl
from jax.experimental.pallas import tpu as pltpu
from jax.sharding import PartitionSpec as P

RANK = 128
FOLDS = 4
H = 4
CX = 16
CY = 32


def padded(x, sides, width):
    for axis, dim in sides:
        count, length = (lax.axis_size(axis), x.shape[dim])
        up = [(i, (i + 1) % count) for i in range(count - 1)]
        down = [(j, i) for i, j in up]
        last = lax.slice_in_dim(x, length - width, length, axis=dim)
        initial = lax.slice_in_dim(x, 0, width, axis=dim)
        before = lax.ppermute(last, axis, up)
        after = lax.ppermute(initial, axis, down)
        x = jnp.concatenate([before, x, after], axis=dim)
    return x


def unpack(bits):
    shifts = jnp.arange(16, dtype=jnp.int32)
    flags = jnp.bitwise_and(lax.shift_right_logical(bits[:, :, None], shifts[None, None, :]), 1)
    return flags.reshape(bits.shape[0], -1).astype(jnp.float32)


def chol_right(cross, gram):
    chol = jnp.linalg.cholesky(gram)
    first = lax.linalg.triangular_solve(chol, cross, left_side=False, lower=True, transpose_a=True)
    return lax.linalg.triangular_solve(chol, first, left_side=False, lower=True, transpose_a=False)


def local(acq_traces, route_owner, route_row, route_fold, sample_bits, left_factors, right_factors):
    n_long = lax.axis_size("mlong")
    n_short = lax.axis_size("mshort")
    peers = n_long * n_short
    rows = acq_traces.shape[0]
    width = acq_traces.shape[1]
    cap = rows // peers
    total = peers * cap
    grid_bits = sample_bits.reshape(CX, CY, width // 16)
    grid_left = left_factors.reshape(CX, CY, FOLDS * RANK)
    valid = route_owner >= 0
    owner = jnp.where(valid, route_owner, 0)
    onehot = (
        (owner[:, None] == jnp.arange(peers, dtype=jnp.int32)[None, :]) & valid[:, None]
    ).astype(jnp.int32)
    within = jnp.sum(jnp.cumsum(onehot, axis=0) * onehot, axis=1) - 1
    place = jnp.where(valid, owner * cap + within, total)
    source = (
        jnp.full((total,), rows, jnp.int32)
        .at[place]
        .set(jnp.arange(rows, dtype=jnp.int32), mode="drop")
    )
    filled_slot = source < rows
    pick = jnp.minimum(source, rows - 1)
    send_traces = jnp.where(
        filled_slot[:, None], jnp.take(acq_traces, pick, axis=0), jnp.zeros((), jnp.bfloat16)
    )
    send_rows = jnp.where(filled_slot, jnp.take(route_row, pick), -1)
    send_folds = jnp.where(filled_slot, jnp.take(route_fold, pick), -1)
    got_traces, got_rows, got_folds = (
        lax.all_to_all(send_traces, ("mlong", "mshort"), split_axis=0, concat_axis=0, tiled=True),
        lax.all_to_all(send_rows, ("mlong", "mshort"), split_axis=0, concat_axis=0, tiled=True),
        lax.all_to_all(send_folds, ("mlong", "mshort"), split_axis=0, concat_axis=0, tiled=True),
    )
    arrival = (
        jnp.full((rows,), total, jnp.int32)
        .at[jnp.where(got_rows >= 0, got_rows, rows)]
        .set(jnp.arange(total, dtype=jnp.int32), mode="drop")
    )
    present = arrival < total
    slot_at = jnp.minimum(arrival, total - 1)
    data = jnp.where(
        present[:, None], jnp.take(got_traces, slot_at, axis=0), jnp.zeros((), jnp.bfloat16)
    )
    fold = jnp.where(present, jnp.take(got_folds, slot_at), -1)
    wide_data, wide_bits, wide_fold, wide_left = (
        padded(data.reshape(CX, CY, width), (("mlong", 0), ("mshort", 1)), H),
        padded(grid_bits, (("mlong", 0), ("mshort", 1)), H),
        padded(fold.reshape(CX, CY), (("mlong", 0), ("mshort", 1)), H),
        padded(grid_left, (("mlong", 0), ("mshort", 1)), H),
    )
    d_win = wide_data.reshape(-1, width)
    f_win = wide_fold.reshape(-1)
    l_win = wide_left.reshape(-1, FOLDS, RANK)
    seen = unpack(wide_bits.reshape(-1, width // 16)) * (f_win >= 0)[:, None].astype(jnp.float32)
    s_core = unpack(sample_bits) * (fold >= 0)[:, None].astype(jnp.float32)
    ridge = jnp.eye(RANK, dtype=jnp.float32)
    updates = []
    chosen = jnp.zeros((rows, width), jnp.float32)
    for f in range(FOLDS):
        factor = l_win[:, f]
        pred = jnp.dot(factor, right_factors[f].T, preferred_element_type=jnp.float32)
        train = seen * (f_win != f)[:, None].astype(jnp.float32)
        imputed = (train * d_win.astype(jnp.float32) + (1.0 - train) * pred).astype(jnp.bfloat16)
        cross = jnp.dot(imputed.T, factor, preferred_element_type=jnp.float32)
        gram = jnp.dot(factor.T, factor, preferred_element_type=jnp.float32) + ridge
        update = chol_right(cross, gram)
        updates.append(update)
        core_pred = jnp.dot(
            left_factors[:, f], update.astype(jnp.bfloat16).T, preferred_element_type=jnp.float32
        )
        chosen = chosen + (fold == f)[:, None].astype(jnp.float32) * core_pred
    new_right = jnp.stack(updates)
    resid = (s_core * (data.astype(jnp.float32) - chosen)).astype(jnp.bfloat16)
    back = jnp.where(
        (got_rows >= 0)[:, None],
        jnp.take(resid, jnp.maximum(got_rows, 0), axis=0),
        jnp.zeros((), jnp.bfloat16),
    )
    returned = lax.all_to_all(back, ("mlong", "mshort"), split_axis=0, concat_axis=0, tiled=True)
    trace_residuals = jnp.where(
        valid[:, None],
        jnp.take(returned, jnp.minimum(place, total - 1), axis=0),
        jnp.zeros((), jnp.bfloat16),
    )
    return (new_right, trace_residuals)


MESH = pl.DeviceIdType.MESH
WIN = 1024
CORE = CX * CY
WIDE = FOLDS * RANK
PARTS = 4
NT = (((1,), (1,)), ((), ()))
HALO = (
    (1, 0, False, CORE - H * CY, CORE, H * CY),
    (-1, 0, False, 0, CORE + H * CY, H * CY),
    (0, 1, True, H * CX, CORE + 2 * H * CY, H * CX),
    (0, -1, True, 0, CORE + 2 * H * CY + H * CX, H * CX),
    (1, 1, True, 2 * H * CX + 48, CORE + 2 * H * (CX + CY), 16),
    (1, -1, True, 2 * H * CX + 32, CORE + 2 * H * (CX + CY) + 16, 16),
    (-1, 1, True, 2 * H * CX + 16, CORE + 2 * H * (CX + CY) + 32, 16),
    (-1, -1, True, 2 * H * CX, CORE + 2 * H * (CX + CY) + 48, 16),
)
PACK = 2 * H * CX + 64


def iota(shape, dim):
    return lax.broadcasted_iota(jnp.int32, shape, dim)


def flags(mask, dtype=jnp.bfloat16):
    return jnp.where(mask, 1.0, 0.0).astype(dtype)


def dot(a, b, dims=(((1,), (0,)), ((), ())), precision=None):
    return lax.dot_general(a, b, dims, precision=precision, preferred_element_type=jnp.float32)


def packed_rows(shape):
    t = iota(shape, 0)
    u = t - 2 * H * CX
    side = jnp.where(t < H * CX, 0, CY - H)
    v = jnp.where(t < H * CX, t, t - H * CX)
    edge = (v // H) * CY + v % H + side
    k = u // 16
    w = u % 16
    corner = (w // H + jnp.where(k >= 2, CX - H, 0)) * CY + w % H + jnp.where(k % 2 == 1, CY - H, 0)
    return jnp.where(u < 0, edge, corner)


def kernel(
    n_long, n_short, traces, own, row, fold, side, right, news, out,
    lw, lpack, fw, fpack, dw, dpack, meta_out, meta_in, send, got, ret, back, pred, kind, cross, lt, gram, umat, vmat, qmat, csel,
    meta_s, meta_r, data_s, data_r, ret_s, ret_r, hl_s, hl_r, hf_s, hf_r, hd_s, hd_r,
):
    peers = n_long * n_short
    cap = CORE // peers
    a = lax.axis_index("mlong")
    c = lax.axis_index("mshort")
    me = a * n_short + c
    width = traces.shape[1]

    lw[0:CORE, :] = side[...]
    lw[CORE:WIN, :] = jnp.zeros((WIN - CORE, WIDE + 128), jnp.bfloat16)
    fw[CORE:WIN, :] = jnp.zeros((WIN - CORE, 128), jnp.bfloat16)
    dw[CORE:WIN, :] = jnp.zeros((WIN - CORE, width), jnp.bfloat16)
    part = width // PARTS

    barrier = pltpu.get_barrier_semaphore()

    def greet(k, carry):
        q = lax.rem(me + k, peers)
        pl.semaphore_signal(barrier, inc=1, device_id=(q // n_short, lax.rem(q, n_short)), device_id_type=MESH)
        return carry

    lax.fori_loop(1, peers, greet, 0)

    pick = flags(packed_rows((PACK, CORE)) == iota((PACK, CORE), 1))
    lpack[...] = dot(pick, side[...]).astype(jnp.bfloat16)

    owner = own[...]
    oh = flags(iota((peers, CORE), 0) == owner, jnp.float32)
    tri = flags(iota((CORE, CORE), 0) < iota((CORE, CORE), 1))
    cum = dot(oh.astype(jnp.bfloat16), tri)
    within = jnp.sum(oh * cum, axis=0, keepdims=True).astype(jnp.int32)
    place = jnp.where(owner >= 0, owner * cap + within, -1)
    rows = row[...]
    vals = [(rows // 128).astype(jnp.float32), (rows % 128).astype(jnp.float32), (fold[...] + 1).astype(jnp.float32)]
    left = jnp.concatenate([oh * v for v in vals], axis=1).astype(jnp.bfloat16)
    rightm = jnp.concatenate([flags(iota((128, CORE), 0) == within + 32 * i) for i in range(3)], axis=1)
    meta = dot(left, rightm, NT)
    for p in range(peers):
        meta_out[p] = meta[p : p + 1, :]
    meta_in[me] = meta_out[me]

    pl.semaphore_wait(barrier, peers - 1)

    def halo(buffer, pack, send_sem, recv_sem, at, span, i):
        da, dc, packed, start, dst, count = HALO[i]
        here = pack if packed else buffer
        return pltpu.make_async_remote_copy(
            src_ref=here.at[pl.ds(start, count), pl.ds(at * span, span)],
            dst_ref=buffer.at[pl.ds(dst, count), pl.ds(at * span, span)],
            send_sem=send_sem.at[at, i],
            recv_sem=recv_sem.at[at, i],
            device_id=(a + da, c + dc),
            device_id_type=MESH,
        )

    def inside(da, dc):
        return (a + da >= 0) & (a + da < n_long) & (c + dc >= 0) & (c + dc < n_short)

    def halo_start(*refs):
        for i in range(8):
            @pl.when(inside(HALO[i][0], HALO[i][1]))
            def _():
                halo(*refs, i).start()

    def halo_recv(*refs):
        for i in range(8):
            @pl.when(inside(-HALO[i][0], -HALO[i][1]))
            def _():
                halo(*refs, i).wait_recv()

    def halo_sent(*refs):
        for i in range(8):
            @pl.when(inside(HALO[i][0], HALO[i][1]))
            def _():
                halo(*refs, i).wait_send()

    def swap(src, dst, send_sem, recv_sem, at, span, k):
        to = lax.rem(me + k, peers)
        return pltpu.make_async_remote_copy(
            src_ref=src.at[to, :, pl.ds(at * span, span)],
            dst_ref=dst.at[me, :, pl.ds(at * span, span)],
            send_sem=send_sem.at[at, k],
            recv_sem=recv_sem.at[at, k],
            device_id=(to // n_short, lax.rem(to, n_short)),
            device_id_type=MESH,
        )

    def arriving(src, dst, send_sem, recv_sem, at, span, k):
        origin = lax.rem(me + peers - k, peers)
        return pltpu.make_async_remote_copy(
            src_ref=src.at[origin, :, pl.ds(at * span, span)],
            dst_ref=dst.at[origin, :, pl.ds(at * span, span)],
            send_sem=send_sem.at[at, k],
            recv_sem=recv_sem.at[at, k],
            device_id=(origin // n_short, lax.rem(origin, n_short)),
            device_id_type=MESH,
        )

    def swap_start(*refs):
        def go(k, carry):
            swap(*refs, k).start()
            return carry

        lax.fori_loop(1, peers, go, 0)

    def swap_recv(*refs):
        def go(k, carry):
            arriving(*refs, k).wait_recv()
            return carry

        lax.fori_loop(1, peers, go, 0)

    def swap_sent(*refs):
        def go(k, carry):
            swap(*refs, k).wait_send()
            return carry

        lax.fori_loop(1, peers, go, 0)

    metas = (meta_out, meta_in, meta_s, meta_r, 0, 128)
    datas = [(send, got, data_s, data_r, at, part) for at in range(PARTS)]
    rets = [(back, ret, ret_s, ret_r, at, part) for at in range(PARTS)]
    lefts = (lw, lpack, hl_s, hl_r, 0, WIDE + 128)
    folds = (fw, fpack, hf_s, hf_r, 0, 128)
    halos = [(dw, dpack, hd_s, hd_r, at, part) for at in range(PARTS)]
    halo_start(*lefts)
    swap_start(*metas)

    def spread(t, carry):
        take = flags(iota((128, CORE), 0) + t * 128 == place)
        block = dot(take, traces[...]).astype(jnp.bfloat16)
        send[pl.ds(t * (128 // cap), 128 // cap)] = block.reshape(128 // cap, cap, width)
        return carry

    lax.fori_loop(0, CORE // 128, spread, 0)
    got[me] = send[me]
    for at in range(PARTS):
        swap_start(*datas[at])

    eye = iota((CORE, CORE), 0) == iota((CORE, CORE), 1)

    def column(line):
        return jnp.sum(jnp.where(eye, line.astype(jnp.float32), 0.0), axis=1, keepdims=True).astype(jnp.int32)

    qmat[...] = flags(column(place) == iota((CORE, CORE), 1))

    swap_recv(*metas)
    meta_got = meta_in[:, 0, :].astype(jnp.bfloat16)
    mine = iota((peers, CORE), 0) == iota((peers, CORE), 1) // cap
    lines = []
    for i in range(3):
        place_of = flags(iota((128, CORE), 0) == iota((128, CORE), 1) % cap + 32 * i)
        lines.append(jnp.sum(jnp.where(mine, dot(meta_got, place_of), 0.0), axis=0, keepdims=True))
    got_row = jnp.where(lines[2] > 0.5, lines[0] * 128.0 + lines[1], -1.0).astype(jnp.int32)
    got_fold = jnp.broadcast_to(lines[2], (128, CORE)).astype(jnp.bfloat16)
    umat[0:CORE, :] = flags(iota((CORE, CORE), 0) == got_row)
    umat[CORE : CORE + PACK, :] = flags(packed_rows((PACK, CORE)) == got_row)
    fw[0:CORE, :] = dot(umat[0:CORE, :], got_fold, NT).astype(jnp.bfloat16)
    fpack[...] = dot(umat[CORE : CORE + PACK, :], got_fold, NT).astype(jnp.bfloat16)
    halo_start(*folds)
    vmat[...] = flags(column(got_row) == iota((CORE, CORE), 1))
    for f in range(FOLDS):
        fs = slice(f * RANK, (f + 1) * RANK)
        csel[:, fs] = jnp.where(fw[0:CORE, :] == f + 1.0, side[:, fs], jnp.zeros((CORE, RANK), jnp.bfloat16))

    halo_recv(*lefts)
    for f in range(FOLDS):
        factor = lw[:, f * RANK : (f + 1) * RANK]
        lt[f] = factor.T
        ident = flags(iota((RANK, RANK), 0) == iota((RANK, RANK), 1), jnp.float32)
        gram[f] = dot(lt[f], factor) + ident

    def eliminate(b, carry):
        k0 = pl.multiple_of(b * 8, 8)
        panel = gram[:, pl.ds(k0, 8), :]
        first = panel
        lane = iota((FOLDS, 8, RANK), 2)
        sub = iota((FOLDS, 8, RANK), 1)
        for j in range(8):
            col = jnp.sum(jnp.where(lane == k0 + j, panel, 0.0), axis=2, keepdims=True)
            inv = 1.0 / col[:, j : j + 1, :]
            w = jnp.where(lane[:, 0:1, :] == k0 + j, inv, panel[:, j : j + 1, :] * inv)
            panel = jnp.where(sub == j, w, jnp.where(lane == k0 + j, 0.0, panel) - col * w)
        signed = jnp.where(lane < k0, -first, first)
        cols = iota((RANK, RANK), 1)
        for f in range(FOLDS):
            change = dot(signed[f].T, panel[f], precision=lax.Precision.HIGHEST)
            gram[f] = jnp.where((cols >= k0) & (cols < k0 + 8), 0.0, gram[f]) - change
        gram[:, pl.ds(k0, 8), :] = panel
        return carry

    lax.fori_loop(0, RANK // 8, eliminate, 0)

    halo_recv(*folds)
    words = iota((128, width), 0)
    offs = iota((128, width), 1)
    expand = flags(words == offs // 16 + jnp.where(offs % 16 >= 8, 64, 0))

    def masks(t, carry):
        r = pl.ds(pl.multiple_of(t * 128, 128), 128)
        byte = dot(lw[r, WIDE : WIDE + 128], expand).astype(jnp.int32)
        bit = lax.shift_right_logical(byte, iota((128, width), 1) % 8) & 1
        flag = bit.astype(jnp.float32).astype(jnp.bfloat16)
        kind[r, :] = jnp.concatenate([fw[r, :]] * (width // 128), axis=1) * flag
        return carry

    lax.fori_loop(0, WIN // 128, masks, 0)

    def collect(at):
        swap_recv(*datas[at])
        cols = slice(at * part, (at + 1) * part)

        def gather(t, carry):
            r = pl.ds(pl.multiple_of(t * 128, 128), 128)
            dw[r, cols] = dot(umat[r, :], got[:, :, cols].reshape(CORE, part)).astype(jnp.bfloat16)
            return carry

        dpack[:, cols] = dot(umat[CORE : CORE + PACK, :], got[:, :, cols].reshape(CORE, part)).astype(jnp.bfloat16)
        lax.fori_loop(0, CORE // 128, gather, 0)
        halo_start(*halos[at])

    def finish(at):
        cols = slice(at * part, (at + 1) * part)
        halo_recv(*halos[at])
        newb = []
        for f in range(FOLDS):
            sort = kind[:, cols]
            train = (sort > 0.5) & (sort != f + 1.0)
            filled = jnp.where(train, dw[:, cols], pred[f, :, cols])
            total = dot(lt[f], filled)
            update = dot(gram[f], total, precision=lax.Precision.HIGHEST)
            cross[f, :, cols] = update
            newb.append(update.astype(jnp.bfloat16))
        chosen = dot(csel[...], jnp.concatenate(newb, axis=0))
        live = kind[0:CORE, cols].astype(jnp.float32) > 0.5
        diff = dw[0:CORE, cols].astype(jnp.float32) - chosen
        resid = jnp.where(live, diff, 0.0).astype(jnp.bfloat16)
        block = dot(vmat[...], resid).astype(jnp.bfloat16)
        back[:, :, cols] = block.reshape(peers, cap, part)
        ret[me, :, cols] = back[me, :, cols]
        swap_start(*rets[at])

    def deliver(at):
        cols = slice(at * part, (at + 1) * part)
        swap_recv(*rets[at])
        out[:, cols] = dot(qmat[...], ret[:, :, cols].reshape(CORE, part)).astype(jnp.bfloat16)

    collect(0)

    for f in range(FOLDS):
        def predict(t, carry, f=f):
            r = pl.ds(pl.multiple_of(t * 128, 128), 128)
            pred[f, r, :] = dot(lw[r, f * RANK : (f + 1) * RANK], right[f], NT).astype(jnp.bfloat16)
            return carry

        lax.fori_loop(0, WIN // 128, predict, 0)

    collect(1)
    for at in range(PARTS):
        finish(at)
        if at + 2 < PARTS:
            collect(at + 2)

    for f in range(FOLDS):
        news[f] = cross[f].T

    for at in range(PARTS):
        deliver(at)

    swap_sent(*metas)
    halo_sent(*lefts)
    halo_sent(*folds)
    for at in range(PARTS):
        swap_sent(*datas[at])
        swap_sent(*rets[at])
        halo_sent(*halos[at])


def fused(acq_traces, route_owner, route_row, route_fold, sample_bits, left_factors, right_factors):
    n_long = lax.axis_size("mlong")
    n_short = lax.axis_size("mshort")
    peers = n_long * n_short
    rows, width = acq_traces.shape
    cap = rows // peers
    low = jnp.bitwise_and(sample_bits, 255).astype(jnp.bfloat16)
    high = lax.shift_right_logical(sample_bits, 8).astype(jnp.bfloat16)
    side = jnp.concatenate([left_factors.reshape(rows, WIDE), low, high], axis=1)
    vmem = pl.BlockSpec(memory_space=pltpu.VMEM)
    bf = jnp.bfloat16
    dma = pltpu.SemaphoreType.DMA
    return pl.pallas_call(
        functools.partial(kernel, n_long, n_short),
        out_shape=(
            jax.ShapeDtypeStruct((FOLDS, width, RANK), jnp.float32),
            jax.ShapeDtypeStruct((rows, width), bf),
        ),
        in_specs=[vmem] * 6,
        out_specs=(vmem, vmem),
        scratch_shapes=[
            pltpu.VMEM((WIN, WIDE + 128), bf),
            pltpu.VMEM((PACK, WIDE + 128), bf),
            pltpu.VMEM((WIN, 128), bf),
            pltpu.VMEM((PACK, 128), bf),
            pltpu.VMEM((WIN, width), bf),
            pltpu.VMEM((PACK, width), bf),
            pltpu.VMEM((peers, 1, 128), jnp.float32),
            pltpu.VMEM((peers, 1, 128), jnp.float32),
            pltpu.VMEM((peers, cap, width), bf),
            pltpu.VMEM((peers, cap, width), bf),
            pltpu.VMEM((peers, cap, width), bf),
            pltpu.VMEM((peers, cap, width), bf),
            pltpu.VMEM((FOLDS, WIN, width), bf),
            pltpu.VMEM((WIN, width), bf),
            pltpu.VMEM((FOLDS, RANK, width), jnp.float32),
            pltpu.VMEM((FOLDS, RANK, WIN), bf),
            pltpu.VMEM((FOLDS, RANK, RANK), jnp.float32),
            pltpu.VMEM((CORE + PACK, CORE), bf),
            pltpu.VMEM((CORE, CORE), bf),
            pltpu.VMEM((CORE, CORE), bf),
            pltpu.VMEM((CORE, WIDE), bf),
            dma((1, peers)), dma((1, peers)), dma((PARTS, peers)), dma((PARTS, peers)), dma((PARTS, peers)), dma((PARTS, peers)),
            dma((1, 8)), dma((1, 8)), dma((1, 8)), dma((1, 8)), dma((PARTS, 8)), dma((PARTS, 8)),
        ],
        compiler_params=pltpu.CompilerParams(
            collective_id=0, has_side_effects=True, vmem_limit_bytes=56 * 1024 * 1024
        ),
    )(
        acq_traces, route_owner.reshape(1, rows), route_row.reshape(1, rows), route_fold.reshape(1, rows),
        side, right_factors,
    )


def solution(mesh):
    in_specs = (
        P(("mlong", "mshort"), None),
        P(("mlong", "mshort")),
        P(("mlong", "mshort")),
        P(("mlong", "mshort")),
        P(("mlong", "mshort"), None),
        P(("mlong", "mshort"), None, None),
        P(None, ("mlong", "mshort"), None),
    )
    out_specs = (P(None, ("mlong", "mshort"), None), P(("mlong", "mshort"), None))
    peers = mesh.shape["mlong"] * mesh.shape["mshort"]
    body = fused if peers * 16 == CX * CY else local
    return jax.shard_map(body, mesh=mesh, in_specs=in_specs, out_specs=out_specs, check_vma=False)
```

```python
import functools

import jax
import jax.numpy as jnp
from jax import lax
from jax.experimental import pallas as pl
from jax.experimental.pallas import tpu as pltpu
from jax.sharding import PartitionSpec as P

RANK = 128
FOLDS = 4
H = 4
CX = 16
CY = 32


def padded(x, sides, width):
    for axis, dim in sides:
        count, length = (lax.axis_size(axis), x.shape[dim])
        up = [(i, (i + 1) % count) for i in range(count - 1)]
        down = [(j, i) for i, j in up]
        last = lax.slice_in_dim(x, length - width, length, axis=dim)
        initial = lax.slice_in_dim(x, 0, width, axis=dim)
        before = lax.ppermute(last, axis, up)
        after = lax.ppermute(initial, axis, down)
        x = jnp.concatenate([before, x, after], axis=dim)
    return x


def unpack(bits):
    shifts = jnp.arange(16, dtype=jnp.int32)
    flags = jnp.bitwise_and(lax.shift_right_logical(bits[:, :, None], shifts[None, None, :]), 1)
    return flags.reshape(bits.shape[0], -1).astype(jnp.float32)


def chol_right(cross, gram):
    chol = jnp.linalg.cholesky(gram)
    first = lax.linalg.triangular_solve(chol, cross, left_side=False, lower=True, transpose_a=True)
    return lax.linalg.triangular_solve(chol, first, left_side=False, lower=True, transpose_a=False)


def local(acq_traces, route_owner, route_row, route_fold, sample_bits, left_factors, right_factors):
    n_long = lax.axis_size("mlong")
    n_short = lax.axis_size("mshort")
    peers = n_long * n_short
    rows = acq_traces.shape[0]
    width = acq_traces.shape[1]
    cap = rows // peers
    total = peers * cap
    grid_bits = sample_bits.reshape(CX, CY, width // 16)
    grid_left = left_factors.reshape(CX, CY, FOLDS * RANK)
    valid = route_owner >= 0
    owner = jnp.where(valid, route_owner, 0)
    onehot = (
        (owner[:, None] == jnp.arange(peers, dtype=jnp.int32)[None, :]) & valid[:, None]
    ).astype(jnp.int32)
    within = jnp.sum(jnp.cumsum(onehot, axis=0) * onehot, axis=1) - 1
    place = jnp.where(valid, owner * cap + within, total)
    source = (
        jnp.full((total,), rows, jnp.int32)
        .at[place]
        .set(jnp.arange(rows, dtype=jnp.int32), mode="drop")
    )
    filled_slot = source < rows
    pick = jnp.minimum(source, rows - 1)
    send_traces = jnp.where(
        filled_slot[:, None], jnp.take(acq_traces, pick, axis=0), jnp.zeros((), jnp.bfloat16)
    )
    send_rows = jnp.where(filled_slot, jnp.take(route_row, pick), -1)
    send_folds = jnp.where(filled_slot, jnp.take(route_fold, pick), -1)
    got_traces, got_rows, got_folds = (
        lax.all_to_all(send_traces, ("mlong", "mshort"), split_axis=0, concat_axis=0, tiled=True),
        lax.all_to_all(send_rows, ("mlong", "mshort"), split_axis=0, concat_axis=0, tiled=True),
        lax.all_to_all(send_folds, ("mlong", "mshort"), split_axis=0, concat_axis=0, tiled=True),
    )
    arrival = (
        jnp.full((rows,), total, jnp.int32)
        .at[jnp.where(got_rows >= 0, got_rows, rows)]
        .set(jnp.arange(total, dtype=jnp.int32), mode="drop")
    )
    present = arrival < total
    slot_at = jnp.minimum(arrival, total - 1)
    data = jnp.where(
        present[:, None], jnp.take(got_traces, slot_at, axis=0), jnp.zeros((), jnp.bfloat16)
    )
    fold = jnp.where(present, jnp.take(got_folds, slot_at), -1)
    wide_data, wide_bits, wide_fold, wide_left = (
        padded(data.reshape(CX, CY, width), (("mlong", 0), ("mshort", 1)), H),
        padded(grid_bits, (("mlong", 0), ("mshort", 1)), H),
        padded(fold.reshape(CX, CY), (("mlong", 0), ("mshort", 1)), H),
        padded(grid_left, (("mlong", 0), ("mshort", 1)), H),
    )
    d_win = wide_data.reshape(-1, width)
    f_win = wide_fold.reshape(-1)
    l_win = wide_left.reshape(-1, FOLDS, RANK)
    seen = unpack(wide_bits.reshape(-1, width // 16)) * (f_win >= 0)[:, None].astype(jnp.float32)
    s_core = unpack(sample_bits) * (fold >= 0)[:, None].astype(jnp.float32)
    ridge = jnp.eye(RANK, dtype=jnp.float32)
    updates = []
    chosen = jnp.zeros((rows, width), jnp.float32)
    for f in range(FOLDS):
        factor = l_win[:, f]
        pred = jnp.dot(factor, right_factors[f].T, preferred_element_type=jnp.float32)
        train = seen * (f_win != f)[:, None].astype(jnp.float32)
        imputed = (train * d_win.astype(jnp.float32) + (1.0 - train) * pred).astype(jnp.bfloat16)
        cross = jnp.dot(imputed.T, factor, preferred_element_type=jnp.float32)
        gram = jnp.dot(factor.T, factor, preferred_element_type=jnp.float32) + ridge
        update = chol_right(cross, gram)
        updates.append(update)
        core_pred = jnp.dot(
            left_factors[:, f], update.astype(jnp.bfloat16).T, preferred_element_type=jnp.float32
        )
        chosen = chosen + (fold == f)[:, None].astype(jnp.float32) * core_pred
    new_right = jnp.stack(updates)
    resid = (s_core * (data.astype(jnp.float32) - chosen)).astype(jnp.bfloat16)
    back = jnp.where(
        (got_rows >= 0)[:, None],
        jnp.take(resid, jnp.maximum(got_rows, 0), axis=0),
        jnp.zeros((), jnp.bfloat16),
    )
    returned = lax.all_to_all(back, ("mlong", "mshort"), split_axis=0, concat_axis=0, tiled=True)
    trace_residuals = jnp.where(
        valid[:, None],
        jnp.take(returned, jnp.minimum(place, total - 1), axis=0),
        jnp.zeros((), jnp.bfloat16),
    )
    return (new_right, trace_residuals)


MESH = pl.DeviceIdType.MESH
WIN = 1024
CORE = CX * CY
WIDE = FOLDS * RANK
PARTS = 4
NT = (((1,), (1,)), ((), ()))
HALO = (
    (1, 0, False, CORE - H * CY, CORE, H * CY),
    (-1, 0, False, 0, CORE + H * CY, H * CY),
    (0, 1, True, H * CX, CORE + 2 * H * CY, H * CX),
    (0, -1, True, 0, CORE + 2 * H * CY + H * CX, H * CX),
    (1, 1, True, 2 * H * CX + 48, CORE + 2 * H * (CX + CY), 16),
    (1, -1, True, 2 * H * CX + 32, CORE + 2 * H * (CX + CY) + 16, 16),
    (-1, 1, True, 2 * H * CX + 16, CORE + 2 * H * (CX + CY) + 32, 16),
    (-1, -1, True, 2 * H * CX, CORE + 2 * H * (CX + CY) + 48, 16),
)
PACK = 2 * H * CX + 64


def iota(shape, dim):
    return lax.broadcasted_iota(jnp.int32, shape, dim)


def flags(mask, dtype=jnp.bfloat16):
    return jnp.where(mask, 1.0, 0.0).astype(dtype)


def dot(a, b, dims=(((1,), (0,)), ((), ())), precision=None):
    return lax.dot_general(a, b, dims, precision=precision, preferred_element_type=jnp.float32)


def div(x, n):
    return lax.shift_right_arithmetic(x, n.bit_length() - 1)


def mod(x, n):
    return x & (n - 1)


def packed_rows(shape):
    t = iota(shape, 0)
    u = t - 2 * H * CX
    v = mod(t, H * CX)
    edge = div(v, H) * CY + mod(v, H) + jnp.where(t < H * CX, 0, CY - H)
    k = div(u, 16)
    w = mod(u, 16)
    corner = (div(w, H) + jnp.where(k >= 2, CX - H, 0)) * CY + mod(w, H) + jnp.where(mod(k, 2) == 1, CY - H, 0)
    return jnp.where(u < 0, edge, corner)


def pieces(x):
    top = x.astype(jnp.bfloat16).astype(jnp.float32)
    rest = x - top
    middle = rest.astype(jnp.bfloat16).astype(jnp.float32)
    return top, middle, rest - middle


def kernel(
    n_long, n_short, traces, own, row, fold, side, right, news, out,
    lw, lpack, fw, fpack, dw, dpack, meta_out, meta_in, send, got, ret, back, pred, kind, cross, lt, gram, umat, vmat, qmat, csel,
    meta_s, meta_r, data_s, data_r, ret_s, ret_r, hl_s, hl_r, hf_s, hf_r, hd_s, hd_r,
):
    peers = n_long * n_short
    cap = CORE // peers
    a = lax.axis_index("mlong")
    c = lax.axis_index("mshort")
    me = a * n_short + c
    width = traces.shape[1]

    lw[0:CORE, :] = side[...]
    lw[CORE:WIN, :] = jnp.zeros((WIN - CORE, WIDE + 128), jnp.bfloat16)
    fw[CORE:WIN, :] = jnp.zeros((WIN - CORE, 128), jnp.bfloat16)
    dw[CORE:WIN, :] = jnp.zeros((WIN - CORE, width), jnp.bfloat16)
    part = width // PARTS

    barrier = pltpu.get_barrier_semaphore()

    def greet(k, carry):
        q = lax.rem(me + k, peers)
        pl.semaphore_signal(barrier, inc=1, device_id=(q // n_short, lax.rem(q, n_short)), device_id_type=MESH)
        return carry

    lax.fori_loop(1, peers, greet, 0)

    owner = own[...]
    oh = flags(iota((peers, CORE), 0) == owner, jnp.float32)
    tri = flags(iota((CORE, CORE), 0) < iota((CORE, CORE), 1))
    cum = dot(oh.astype(jnp.bfloat16), tri)
    within = jnp.sum(oh * cum, axis=0, keepdims=True).astype(jnp.int32)
    place = jnp.where(owner >= 0, owner * cap + within, -1)
    rows = row[...]
    vals = [div(rows, 128).astype(jnp.float32), mod(rows, 128).astype(jnp.float32), (fold[...] + 1).astype(jnp.float32)]
    left = jnp.concatenate([oh * v for v in vals], axis=1).astype(jnp.bfloat16)
    rightm = jnp.concatenate([flags(iota((128, CORE), 0) == within + 32 * i) for i in range(3)], axis=1)
    meta = dot(left, rightm, NT)
    for p in range(peers):
        meta_out[p] = meta[p : p + 1, :]
    meta_in[me] = meta_out[me]

    pl.semaphore_wait(barrier, peers - 1)

    def halo(buffer, pack, send_sem, recv_sem, at, span, i):
        da, dc, packed, start, dst, count = HALO[i]
        here = pack if packed else buffer
        return pltpu.make_async_remote_copy(
            src_ref=here.at[pl.ds(start, count), pl.ds(at * span, span)],
            dst_ref=buffer.at[pl.ds(dst, count), pl.ds(at * span, span)],
            send_sem=send_sem.at[at, i],
            recv_sem=recv_sem.at[at, i],
            device_id=(a + da, c + dc),
            device_id_type=MESH,
        )

    def inside(da, dc):
        return (a + da >= 0) & (a + da < n_long) & (c + dc >= 0) & (c + dc < n_short)

    def halo_start(*refs):
        for i in range(8):
            @pl.when(inside(HALO[i][0], HALO[i][1]))
            def _():
                halo(*refs, i).start()

    def halo_recv(*refs):
        for i in range(8):
            @pl.when(inside(-HALO[i][0], -HALO[i][1]))
            def _():
                halo(*refs, i).wait_recv()

    def halo_sent(*refs):
        for i in range(8):
            @pl.when(inside(HALO[i][0], HALO[i][1]))
            def _():
                halo(*refs, i).wait_send()

    def swap(src, dst, send_sem, recv_sem, at, span, k):
        to = lax.rem(me + k, peers)
        return pltpu.make_async_remote_copy(
            src_ref=src.at[to, :, pl.ds(at * span, span)],
            dst_ref=dst.at[me, :, pl.ds(at * span, span)],
            send_sem=send_sem.at[at],
            recv_sem=recv_sem.at[at],
            device_id=(to // n_short, lax.rem(to, n_short)),
            device_id_type=MESH,
        )

    def all_of(src, dst, send_sem, recv_sem, at, span):
        return pltpu.make_async_remote_copy(
            src_ref=src.at[pl.ds(1, peers - 1), :, pl.ds(at * span, span)],
            dst_ref=dst.at[pl.ds(1, peers - 1), :, pl.ds(at * span, span)],
            send_sem=send_sem.at[at],
            recv_sem=recv_sem.at[at],
            device_id=(a, lax.rem(c + 1, n_short)),
            device_id_type=MESH,
        )

    def swap_start(*refs):
        def go(k, carry):
            swap(*refs, k).start()
            return carry

        lax.fori_loop(1, peers, go, 0)

    def swap_recv(*refs):
        all_of(*refs).wait_recv()

    def swap_sent(*refs):
        all_of(*refs).wait_send()

    metas = (meta_out, meta_in, meta_s, meta_r, 0, 128)
    datas = [(send, got, data_s, data_r, at, part) for at in range(PARTS)]
    rets = [(back, ret, ret_s, ret_r, at, part) for at in range(PARTS)]
    lefts = (lw, lpack, hl_s, hl_r, 0, WIDE + 128)
    folds = (fw, fpack, hf_s, hf_r, 0, 128)
    halos = [(dw, dpack, hd_s, hd_r, at, part) for at in range(PARTS)]
    swap_start(*metas)

    take = flags(iota((CORE, CORE), 0) == place)
    for at in range(PARTS):
        cols = slice(at * part, (at + 1) * part)
        send[:, :, cols] = dot(take, traces[:, cols]).astype(jnp.bfloat16).reshape(peers, cap, part)
        swap_start(*datas[at])
    got[me] = send[me]

    pick = flags(packed_rows((PACK, CORE)) == iota((PACK, CORE), 1))
    lpack[...] = dot(pick, side[...]).astype(jnp.bfloat16)
    halo_start(*lefts)

    eye = iota((CORE, CORE), 0) == iota((CORE, CORE), 1)

    def column(line):
        return jnp.sum(jnp.where(eye, line.astype(jnp.float32), 0.0), axis=1, keepdims=True).astype(jnp.int32)

    qmat[...] = flags(column(place) == iota((CORE, CORE), 1))

    swap_recv(*metas)
    meta_got = meta_in[:, 0, :].astype(jnp.bfloat16)
    mine = iota((peers, CORE), 0) == div(iota((peers, CORE), 1), cap)
    lines = []
    for i in range(3):
        place_of = flags(iota((128, CORE), 0) == mod(iota((128, CORE), 1), cap) + 32 * i)
        lines.append(jnp.sum(jnp.where(mine, dot(meta_got, place_of), 0.0), axis=0, keepdims=True))
    got_row = jnp.where(lines[2] > 0.5, lines[0] * 128.0 + lines[1], -1.0).astype(jnp.int32)
    got_fold = jnp.broadcast_to(lines[2], (128, CORE)).astype(jnp.bfloat16)
    umat[0:CORE, :] = flags(iota((CORE, CORE), 0) == got_row)
    umat[CORE : CORE + PACK, :] = flags(packed_rows((PACK, CORE)) == got_row)
    fw[0:CORE, :] = dot(umat[0:CORE, :], got_fold, NT).astype(jnp.bfloat16)
    fpack[...] = dot(umat[CORE : CORE + PACK, :], got_fold, NT).astype(jnp.bfloat16)
    halo_start(*folds)
    vmat[...] = flags(column(got_row) == iota((CORE, CORE), 1))
    for f in range(FOLDS):
        fs = slice(f * RANK, (f + 1) * RANK)
        csel[:, fs] = jnp.where(fw[0:CORE, :] == f + 1.0, side[:, fs], jnp.zeros((CORE, RANK), jnp.bfloat16))

    halo_recv(*lefts)
    for f in range(FOLDS):
        factor = lw[:, f * RANK : (f + 1) * RANK]
        lt[f] = factor.T
        ident = flags(iota((RANK, RANK), 0) == iota((RANK, RANK), 1), jnp.float32)
        gram[f] = dot(lt[f], factor) + ident

    halo_recv(*folds)
    words = iota((128, width), 0)
    offs = iota((128, width), 1)
    expand = flags(words == div(offs, 16) + jnp.where(mod(offs, 16) >= 8, 64, 0))
    steps = RANK // 8
    tall = WIN // steps
    quarter = FOLDS * WIN // steps

    def eliminate(b, carry):
        k0 = pl.multiple_of(b * 8, 8)
        first = gram[:, pl.ds(k0, 8), :]
        lane = iota((FOLDS, 8, RANK), 2)
        sub = iota((FOLDS, 8, RANK), 1)
        inner = (lane >= k0) & (lane < k0 + 8)
        cols = [
            jnp.broadcast_to(jnp.sum(jnp.where(lane == k0 + j, first, 0.0), axis=2, keepdims=True), first.shape)
            for j in range(8)
        ]
        panel = jnp.where(inner, jnp.where(lane - k0 == sub, 1.0, 0.0), first)
        for j in range(8):
            pivot = cols[j]
            inv = 1.0 / pivot[:, j : j + 1, :]

            def reduce_rows(x):
                w = x[:, j : j + 1, :] * inv
                return jnp.where(sub == j, w, x - pivot * w)

            panel = reduce_rows(panel)
            cols = [reduce_rows(x) if i > j else x for i, x in enumerate(cols)]
        signed = jnp.where(lane < k0, -first, first)
        keep = (iota((RANK, RANK), 1) < k0) | (iota((RANK, RANK), 1) >= k0 + 8)
        for f in range(FOLDS):
            a1, a2, a3 = pieces(signed[f])
            b1, b2, b3 = pieces(panel[f])
            lhs = jnp.concatenate([a1, a1, a2, a2, a1, a3, jnp.zeros((80, RANK), jnp.float32)], axis=0).T
            rhs = jnp.concatenate([b1, b2, b1, b2, b3, b1, jnp.zeros((80, RANK), jnp.float32)], axis=0)
            change = dot(lhs.astype(jnp.bfloat16), rhs.astype(jnp.bfloat16))
            gram[f] = jnp.where(keep, gram[f], 0.0) - change
        gram[:, pl.ds(k0, 8), :] = panel

        r = pl.ds(pl.multiple_of(b * tall, tall), tall)
        byte = dot(lw[r, WIDE : WIDE + 128], expand).astype(jnp.int32)
        bit = lax.shift_right_logical(byte, mod(iota((tall, width), 1), 8)) & 1
        flag = bit.astype(jnp.float32).astype(jnp.bfloat16)
        kind[r, :] = jnp.concatenate([fw[r, :]] * (width // 128), axis=1) * flag

        f = b // (steps // FOLDS)
        q = pl.ds(pl.multiple_of(lax.rem(b, steps // FOLDS) * quarter, quarter), quarter)
        left_f = lw[q, pl.ds(pl.multiple_of(f * RANK, RANK), RANK)]
        pred[f, q, :] = dot(left_f, right[f], NT).astype(jnp.bfloat16)
        return carry

    def collect(at):
        swap_recv(*datas[at])
        cols = slice(at * part, (at + 1) * part)

        arrived = got[:, :, cols].reshape(CORE, part)
        dpack[:, cols] = dot(umat[CORE : CORE + PACK, :], arrived).astype(jnp.bfloat16)
        dw[0:CORE, cols] = dot(umat[0:CORE, :], arrived).astype(jnp.bfloat16)
        halo_start(*halos[at])

    def finish(at):
        cols = slice(at * part, (at + 1) * part)
        halo_recv(*halos[at])
        newb = []
        for f in range(FOLDS):
            sort = kind[:, cols]
            train = (sort > 0.5) & (sort != f + 1.0)
            filled = jnp.where(train, dw[:, cols], pred[f, :, cols])
            total = dot(lt[f], filled)
            update = dot(gram[f], total, precision=lax.Precision.HIGHEST)
            cross[f, :, cols] = update
            newb.append(update.astype(jnp.bfloat16))
        chosen = dot(csel[...], jnp.concatenate(newb, axis=0))
        live = kind[0:CORE, cols].astype(jnp.float32) > 0.5
        diff = dw[0:CORE, cols].astype(jnp.float32) - chosen
        resid = jnp.where(live, diff, 0.0).astype(jnp.bfloat16)
        block = dot(vmat[...], resid).astype(jnp.bfloat16)
        back[:, :, cols] = block.reshape(peers, cap, part)
        ret[me, :, cols] = back[me, :, cols]
        swap_start(*rets[at])

    def deliver(at):
        cols = slice(at * part, (at + 1) * part)
        swap_recv(*rets[at])
        out[:, cols] = dot(qmat[...], ret[:, :, cols].reshape(CORE, part)).astype(jnp.bfloat16)

    lax.fori_loop(0, steps // 2, eliminate, 0)
    collect(0)
    lax.fori_loop(steps // 2, steps, eliminate, 0)
    collect(1)
    for at in range(PARTS):
        finish(at)
        if at + 2 < PARTS:
            collect(at + 2)

    for f in range(FOLDS):
        news[f] = cross[f].T

    for at in range(PARTS):
        deliver(at)

    swap_sent(*metas)
    halo_sent(*lefts)
    halo_sent(*folds)
    for at in range(PARTS):
        swap_sent(*datas[at])
        swap_sent(*rets[at])
        halo_sent(*halos[at])


def fused(acq_traces, route_owner, route_row, route_fold, sample_bits, left_factors, right_factors):
    n_long = lax.axis_size("mlong")
    n_short = lax.axis_size("mshort")
    peers = n_long * n_short
    rows, width = acq_traces.shape
    cap = rows // peers
    low = jnp.bitwise_and(sample_bits, 255).astype(jnp.bfloat16)
    high = lax.shift_right_logical(sample_bits, 8).astype(jnp.bfloat16)
    side = jnp.concatenate([left_factors.reshape(rows, WIDE), low, high], axis=1)
    vmem = pl.BlockSpec(memory_space=pltpu.VMEM)
    bf = jnp.bfloat16
    dma = pltpu.SemaphoreType.DMA
    return pl.pallas_call(
        functools.partial(kernel, n_long, n_short),
        out_shape=(
            jax.ShapeDtypeStruct((FOLDS, width, RANK), jnp.float32),
            jax.ShapeDtypeStruct((rows, width), bf),
        ),
        in_specs=[vmem] * 6,
        out_specs=(vmem, vmem),
        scratch_shapes=[
            pltpu.VMEM((WIN, WIDE + 128), bf),
            pltpu.VMEM((PACK, WIDE + 128), bf),
            pltpu.VMEM((WIN, 128), bf),
            pltpu.VMEM((PACK, 128), bf),
            pltpu.VMEM((WIN, width), bf),
            pltpu.VMEM((PACK, width), bf),
            pltpu.VMEM((peers, 1, 128), jnp.float32),
            pltpu.VMEM((peers, 1, 128), jnp.float32),
            pltpu.VMEM((peers, cap, width), bf),
            pltpu.VMEM((peers, cap, width), bf),
            pltpu.VMEM((peers, cap, width), bf),
            pltpu.VMEM((peers, cap, width), bf),
            pltpu.VMEM((FOLDS, WIN, width), bf),
            pltpu.VMEM((WIN, width), bf),
            pltpu.VMEM((FOLDS, RANK, width), jnp.float32),
            pltpu.VMEM((FOLDS, RANK, WIN), bf),
            pltpu.VMEM((FOLDS, RANK, RANK), jnp.float32),
            pltpu.VMEM((CORE + PACK, CORE), bf),
            pltpu.VMEM((CORE, CORE), bf),
            pltpu.VMEM((CORE, CORE), bf),
            pltpu.VMEM((CORE, WIDE), bf),
            dma((1,)), dma((1,)), dma((PARTS,)), dma((PARTS,)), dma((PARTS,)), dma((PARTS,)),
            dma((1, 8)), dma((1, 8)), dma((1, 8)), dma((1, 8)), dma((PARTS, 8)), dma((PARTS, 8)),
        ],
        compiler_params=pltpu.CompilerParams(
            collective_id=0, has_side_effects=True, vmem_limit_bytes=56 * 1024 * 1024
        ),
    )(
        acq_traces, route_owner.reshape(1, rows), route_row.reshape(1, rows), route_fold.reshape(1, rows),
        side, right_factors,
    )


def solution(mesh):
    in_specs = (
        P(("mlong", "mshort"), None),
        P(("mlong", "mshort")),
        P(("mlong", "mshort")),
        P(("mlong", "mshort")),
        P(("mlong", "mshort"), None),
        P(("mlong", "mshort"), None, None),
        P(None, ("mlong", "mshort"), None),
    )
    out_specs = (P(None, ("mlong", "mshort"), None), P(("mlong", "mshort"), None))
    peers = mesh.shape["mlong"] * mesh.shape["mshort"]
    body = fused if peers * 16 == CX * CY else local
    return jax.shard_map(body, mesh=mesh, in_specs=in_specs, out_specs=out_specs, check_vma=False)
```

```python
import functools

import jax
import jax.numpy as jnp
from jax import lax
from jax.experimental import pallas as pl
from jax.experimental.pallas import tpu as pltpu
from jax.sharding import PartitionSpec as P

RANK = 128
FOLDS = 4
H = 4
CX = 16
CY = 32


def padded(x, sides, width):
    for axis, dim in sides:
        count, length = (lax.axis_size(axis), x.shape[dim])
        up = [(i, (i + 1) % count) for i in range(count - 1)]
        down = [(j, i) for i, j in up]
        last = lax.slice_in_dim(x, length - width, length, axis=dim)
        initial = lax.slice_in_dim(x, 0, width, axis=dim)
        before = lax.ppermute(last, axis, up)
        after = lax.ppermute(initial, axis, down)
        x = jnp.concatenate([before, x, after], axis=dim)
    return x


def unpack(bits):
    shifts = jnp.arange(16, dtype=jnp.int32)
    flags = jnp.bitwise_and(lax.shift_right_logical(bits[:, :, None], shifts[None, None, :]), 1)
    return flags.reshape(bits.shape[0], -1).astype(jnp.float32)


def chol_right(cross, gram):
    chol = jnp.linalg.cholesky(gram)
    first = lax.linalg.triangular_solve(chol, cross, left_side=False, lower=True, transpose_a=True)
    return lax.linalg.triangular_solve(chol, first, left_side=False, lower=True, transpose_a=False)


def local(acq_traces, route_owner, route_row, route_fold, sample_bits, left_factors, right_factors):
    n_long = lax.axis_size("mlong")
    n_short = lax.axis_size("mshort")
    peers = n_long * n_short
    rows = acq_traces.shape[0]
    width = acq_traces.shape[1]
    cap = rows // peers
    total = peers * cap
    grid_bits = sample_bits.reshape(CX, CY, width // 16)
    grid_left = left_factors.reshape(CX, CY, FOLDS * RANK)
    valid = route_owner >= 0
    owner = jnp.where(valid, route_owner, 0)
    onehot = (
        (owner[:, None] == jnp.arange(peers, dtype=jnp.int32)[None, :]) & valid[:, None]
    ).astype(jnp.int32)
    within = jnp.sum(jnp.cumsum(onehot, axis=0) * onehot, axis=1) - 1
    place = jnp.where(valid, owner * cap + within, total)
    source = (
        jnp.full((total,), rows, jnp.int32)
        .at[place]
        .set(jnp.arange(rows, dtype=jnp.int32), mode="drop")
    )
    filled_slot = source < rows
    pick = jnp.minimum(source, rows - 1)
    send_traces = jnp.where(
        filled_slot[:, None], jnp.take(acq_traces, pick, axis=0), jnp.zeros((), jnp.bfloat16)
    )
    send_rows = jnp.where(filled_slot, jnp.take(route_row, pick), -1)
    send_folds = jnp.where(filled_slot, jnp.take(route_fold, pick), -1)
    got_traces, got_rows, got_folds = (
        lax.all_to_all(send_traces, ("mlong", "mshort"), split_axis=0, concat_axis=0, tiled=True),
        lax.all_to_all(send_rows, ("mlong", "mshort"), split_axis=0, concat_axis=0, tiled=True),
        lax.all_to_all(send_folds, ("mlong", "mshort"), split_axis=0, concat_axis=0, tiled=True),
    )
    arrival = (
        jnp.full((rows,), total, jnp.int32)
        .at[jnp.where(got_rows >= 0, got_rows, rows)]
        .set(jnp.arange(total, dtype=jnp.int32), mode="drop")
    )
    present = arrival < total
    slot_at = jnp.minimum(arrival, total - 1)
    data = jnp.where(
        present[:, None], jnp.take(got_traces, slot_at, axis=0), jnp.zeros((), jnp.bfloat16)
    )
    fold = jnp.where(present, jnp.take(got_folds, slot_at), -1)
    wide_data, wide_bits, wide_fold, wide_left = (
        padded(data.reshape(CX, CY, width), (("mlong", 0), ("mshort", 1)), H),
        padded(grid_bits, (("mlong", 0), ("mshort", 1)), H),
        padded(fold.reshape(CX, CY), (("mlong", 0), ("mshort", 1)), H),
        padded(grid_left, (("mlong", 0), ("mshort", 1)), H),
    )
    d_win = wide_data.reshape(-1, width)
    f_win = wide_fold.reshape(-1)
    l_win = wide_left.reshape(-1, FOLDS, RANK)
    seen = unpack(wide_bits.reshape(-1, width // 16)) * (f_win >= 0)[:, None].astype(jnp.float32)
    s_core = unpack(sample_bits) * (fold >= 0)[:, None].astype(jnp.float32)
    ridge = jnp.eye(RANK, dtype=jnp.float32)
    updates = []
    chosen = jnp.zeros((rows, width), jnp.float32)
    for f in range(FOLDS):
        factor = l_win[:, f]
        pred = jnp.dot(factor, right_factors[f].T, preferred_element_type=jnp.float32)
        train = seen * (f_win != f)[:, None].astype(jnp.float32)
        imputed = (train * d_win.astype(jnp.float32) + (1.0 - train) * pred).astype(jnp.bfloat16)
        cross = jnp.dot(imputed.T, factor, preferred_element_type=jnp.float32)
        gram = jnp.dot(factor.T, factor, preferred_element_type=jnp.float32) + ridge
        update = chol_right(cross, gram)
        updates.append(update)
        core_pred = jnp.dot(
            left_factors[:, f], update.astype(jnp.bfloat16).T, preferred_element_type=jnp.float32
        )
        chosen = chosen + (fold == f)[:, None].astype(jnp.float32) * core_pred
    new_right = jnp.stack(updates)
    resid = (s_core * (data.astype(jnp.float32) - chosen)).astype(jnp.bfloat16)
    back = jnp.where(
        (got_rows >= 0)[:, None],
        jnp.take(resid, jnp.maximum(got_rows, 0), axis=0),
        jnp.zeros((), jnp.bfloat16),
    )
    returned = lax.all_to_all(back, ("mlong", "mshort"), split_axis=0, concat_axis=0, tiled=True)
    trace_residuals = jnp.where(
        valid[:, None],
        jnp.take(returned, jnp.minimum(place, total - 1), axis=0),
        jnp.zeros((), jnp.bfloat16),
    )
    return (new_right, trace_residuals)


MESH = pl.DeviceIdType.MESH
WIN = 1024
CORE = CX * CY
WIDE = FOLDS * RANK
PARTS = 2
NT = (((1,), (1,)), ((), ()))
HALO = (
    (1, 0, False, CORE - H * CY, CORE, H * CY),
    (-1, 0, False, 0, CORE + H * CY, H * CY),
    (0, 1, True, H * CX, CORE + 2 * H * CY, H * CX),
    (0, -1, True, 0, CORE + 2 * H * CY + H * CX, H * CX),
    (1, 1, True, 2 * H * CX + 48, CORE + 2 * H * (CX + CY), 16),
    (1, -1, True, 2 * H * CX + 32, CORE + 2 * H * (CX + CY) + 16, 16),
    (-1, 1, True, 2 * H * CX + 16, CORE + 2 * H * (CX + CY) + 32, 16),
    (-1, -1, True, 2 * H * CX, CORE + 2 * H * (CX + CY) + 48, 16),
)
PACK = 2 * H * CX + 64


def iota(shape, dim):
    return lax.broadcasted_iota(jnp.int32, shape, dim)


def flags(mask, dtype=jnp.bfloat16):
    return jnp.where(mask, 1.0, 0.0).astype(dtype)


def dot(a, b, dims=(((1,), (0,)), ((), ())), precision=None):
    return lax.dot_general(a, b, dims, precision=precision, preferred_element_type=jnp.float32)


def div(x, n):
    return lax.shift_right_arithmetic(x, n.bit_length() - 1)


def mod(x, n):
    return x & (n - 1)


def packed_rows(shape):
    t = iota(shape, 0)
    u = t - 2 * H * CX
    v = mod(t, H * CX)
    edge = div(v, H) * CY + mod(v, H) + jnp.where(t < H * CX, 0, CY - H)
    k = div(u, 16)
    w = mod(u, 16)
    corner = (div(w, H) + jnp.where(k >= 2, CX - H, 0)) * CY + mod(w, H) + jnp.where(mod(k, 2) == 1, CY - H, 0)
    return jnp.where(u < 0, edge, corner)


def pieces(x):
    top = x.astype(jnp.bfloat16).astype(jnp.float32)
    rest = x - top
    middle = rest.astype(jnp.bfloat16).astype(jnp.float32)
    return top, middle, rest - middle


def kernel(
    n_long, n_short, traces, own, row, fold, side, right, news, out,
    lw, lpack, fw, fpack, dw, dpack, meta_out, meta_in, send, got, ret, back, pred, kind, cross, lt, gram, umat, vmat, qmat, csel,
    meta_s, meta_r, data_s, data_r, ret_s, ret_r, hl_s, hl_r, hf_s, hf_r, hd_s, hd_r,
):
    peers = n_long * n_short
    cap = CORE // peers
    a = lax.axis_index("mlong")
    c = lax.axis_index("mshort")
    me = a * n_short + c
    width = traces.shape[1]

    lw[0:CORE, :] = side[...]
    lw[CORE:WIN, :] = jnp.zeros((WIN - CORE, WIDE + 128), jnp.bfloat16)
    fw[CORE:WIN, :] = jnp.zeros((WIN - CORE, 128), jnp.bfloat16)
    dw[CORE:WIN, :] = jnp.zeros((WIN - CORE, width), jnp.bfloat16)
    part = width // PARTS

    barrier = pltpu.get_barrier_semaphore()

    others = [None]
    for k in range(1, peers):
        q = lax.rem(me + k, peers)
        others.append((q, (q // n_short, lax.rem(q, n_short))))
        pl.semaphore_signal(barrier, inc=1, device_id=others[k][1], device_id_type=MESH)

    owner = own[...]
    oh = flags(iota((peers, CORE), 0) == owner, jnp.float32)
    tri = flags(iota((CORE, CORE), 0) < iota((CORE, CORE), 1))
    cum = dot(oh.astype(jnp.bfloat16), tri)
    within = jnp.sum(oh * cum, axis=0, keepdims=True).astype(jnp.int32)
    place = jnp.where(owner >= 0, owner * cap + within, -1)
    rows = row[...]
    vals = [div(rows, 128).astype(jnp.float32), mod(rows, 128).astype(jnp.float32), (fold[...] + 1).astype(jnp.float32)]
    left = jnp.concatenate([oh * v for v in vals], axis=1).astype(jnp.bfloat16)
    rightm = jnp.concatenate([flags(iota((128, CORE), 0) == within + 32 * i) for i in range(3)], axis=1)
    meta = dot(left, rightm, NT)
    for p in range(peers):
        meta_out[p] = meta[p : p + 1, :]
    meta_in[me] = meta_out[me]

    pl.semaphore_wait(barrier, peers - 1)

    def halo(buffer, pack, send_sem, recv_sem, at, span, i):
        da, dc, packed, start, dst, count = HALO[i]
        here = pack if packed else buffer
        return pltpu.make_async_remote_copy(
            src_ref=here.at[pl.ds(start, count), pl.ds(at * span, span)],
            dst_ref=buffer.at[pl.ds(dst, count), pl.ds(at * span, span)],
            send_sem=send_sem.at[at, i],
            recv_sem=recv_sem.at[at, i],
            device_id=(a + da, c + dc),
            device_id_type=MESH,
        )

    def inside(da, dc):
        return (a + da >= 0) & (a + da < n_long) & (c + dc >= 0) & (c + dc < n_short)

    def halo_start(*refs):
        for i in range(8):
            @pl.when(inside(HALO[i][0], HALO[i][1]))
            def _():
                halo(*refs, i).start()

    def halo_recv(*refs):
        for i in range(8):
            @pl.when(inside(-HALO[i][0], -HALO[i][1]))
            def _():
                halo(*refs, i).wait_recv()

    def halo_sent(*refs):
        for i in range(8):
            @pl.when(inside(HALO[i][0], HALO[i][1]))
            def _():
                halo(*refs, i).wait_send()

    def swap(src, dst, send_sem, recv_sem, at, span, k):
        to, place_of_to = others[k]
        return pltpu.make_async_remote_copy(
            src_ref=src.at[to, :, pl.ds(at * span, span)],
            dst_ref=dst.at[me, :, pl.ds(at * span, span)],
            send_sem=send_sem.at[at],
            recv_sem=recv_sem.at[at],
            device_id=place_of_to,
            device_id_type=MESH,
        )

    def all_of(src, dst, send_sem, recv_sem, at, span):
        return pltpu.make_async_remote_copy(
            src_ref=src.at[pl.ds(1, peers - 1), :, pl.ds(at * span, span)],
            dst_ref=dst.at[pl.ds(1, peers - 1), :, pl.ds(at * span, span)],
            send_sem=send_sem.at[at],
            recv_sem=recv_sem.at[at],
            device_id=(a, lax.rem(c + 1, n_short)),
            device_id_type=MESH,
        )

    def swap_start(*refs):
        for k in range(1, peers):
            swap(*refs, k).start()

    def swap_recv(*refs):
        all_of(*refs).wait_recv()

    def swap_sent(*refs):
        all_of(*refs).wait_send()

    metas = (meta_out, meta_in, meta_s, meta_r, 0, 128)
    datas = [(send, got, data_s, data_r, at, part) for at in range(PARTS)]
    rets = [(back, ret, ret_s, ret_r, at, part) for at in range(PARTS)]
    lefts = (lw, lpack, hl_s, hl_r, 0, WIDE + 128)
    folds = (fw, fpack, hf_s, hf_r, 0, 128)
    halos = [(dw, dpack, hd_s, hd_r, at, part) for at in range(PARTS)]
    swap_start(*metas)

    take = flags(iota((CORE, CORE), 0) == place)
    for at in range(PARTS):
        cols = slice(at * part, (at + 1) * part)
        send[:, :, cols] = dot(take, traces[:, cols]).astype(jnp.bfloat16).reshape(peers, cap, part)
        swap_start(*datas[at])
    got[me] = send[me]

    pick = flags(packed_rows((PACK, CORE)) == iota((PACK, CORE), 1))
    lpack[...] = dot(pick, side[...]).astype(jnp.bfloat16)
    halo_start(*lefts)

    eye = iota((CORE, CORE), 0) == iota((CORE, CORE), 1)

    def column(line):
        return jnp.sum(jnp.where(eye, line.astype(jnp.float32), 0.0), axis=1, keepdims=True).astype(jnp.int32)

    qmat[...] = flags(column(place) == iota((CORE, CORE), 1))

    swap_recv(*metas)
    meta_got = meta_in[:, 0, :].astype(jnp.bfloat16)
    mine = iota((peers, CORE), 0) == div(iota((peers, CORE), 1), cap)
    lines = []
    for i in range(3):
        place_of = flags(iota((128, CORE), 0) == mod(iota((128, CORE), 1), cap) + 32 * i)
        lines.append(jnp.sum(jnp.where(mine, dot(meta_got, place_of), 0.0), axis=0, keepdims=True))
    got_row = jnp.where(lines[2] > 0.5, lines[0] * 128.0 + lines[1], -1.0).astype(jnp.int32)
    got_fold = jnp.broadcast_to(lines[2], (128, CORE)).astype(jnp.bfloat16)
    umat[0:CORE, :] = flags(iota((CORE, CORE), 0) == got_row)
    umat[CORE : CORE + PACK, :] = flags(packed_rows((PACK, CORE)) == got_row)
    fw[0:CORE, :] = dot(umat[0:CORE, :], got_fold, NT).astype(jnp.bfloat16)
    fpack[...] = dot(umat[CORE : CORE + PACK, :], got_fold, NT).astype(jnp.bfloat16)
    halo_start(*folds)
    vmat[...] = flags(column(got_row) == iota((CORE, CORE), 1))
    for f in range(FOLDS):
        fs = slice(f * RANK, (f + 1) * RANK)
        csel[:, fs] = jnp.where(fw[0:CORE, :] == f + 1.0, side[:, fs], jnp.zeros((CORE, RANK), jnp.bfloat16))

    halo_recv(*lefts)
    for f in range(FOLDS):
        factor = lw[:, f * RANK : (f + 1) * RANK]
        lt[f] = factor.T
        ident = flags(iota((RANK, RANK), 0) == iota((RANK, RANK), 1), jnp.float32)
        gram[f] = dot(lt[f], factor) + ident

    halo_recv(*folds)
    words = iota((128, width), 0)
    offs = iota((128, width), 1)
    expand = flags(words == div(offs, 16) + jnp.where(mod(offs, 16) >= 8, 64, 0))
    steps = RANK // 8
    tall = WIN // steps
    quarter = FOLDS * WIN // steps

    def eliminate(b, carry):
        k0 = pl.multiple_of(b * 8, 8)
        first = gram[:, pl.ds(k0, 8), :]
        lane = iota((FOLDS, 8, RANK), 2)
        sub = iota((FOLDS, 8, RANK), 1)
        inner = (lane >= k0) & (lane < k0 + 8)
        cols = [
            jnp.broadcast_to(jnp.sum(jnp.where(lane == k0 + j, first, 0.0), axis=2, keepdims=True), first.shape)
            for j in range(8)
        ]
        panel = jnp.where(inner, jnp.where(lane - k0 == sub, 1.0, 0.0), first)
        for j in range(8):
            pivot = cols[j]
            inv = 1.0 / pivot[:, j : j + 1, :]

            def reduce_rows(x):
                w = x[:, j : j + 1, :] * inv
                return jnp.where(sub == j, w, x - pivot * w)

            panel = reduce_rows(panel)
            cols = [reduce_rows(x) if i > j else x for i, x in enumerate(cols)]
        signed = jnp.where(lane < k0, -first, first)
        keep = (iota((RANK, RANK), 1) < k0) | (iota((RANK, RANK), 1) >= k0 + 8)
        for f in range(FOLDS):
            a1, a2, a3 = pieces(signed[f])
            b1, b2, b3 = pieces(panel[f])
            lhs = jnp.concatenate([a1, a1, a2, a2, a1, a3, jnp.zeros((80, RANK), jnp.float32)], axis=0).T
            rhs = jnp.concatenate([b1, b2, b1, b2, b3, b1, jnp.zeros((80, RANK), jnp.float32)], axis=0)
            change = dot(lhs.astype(jnp.bfloat16), rhs.astype(jnp.bfloat16))
            gram[f] = jnp.where(keep, gram[f], 0.0) - change
        gram[:, pl.ds(k0, 8), :] = panel

        r = pl.ds(pl.multiple_of(b * tall, tall), tall)
        byte = dot(lw[r, WIDE : WIDE + 128], expand).astype(jnp.int32)
        bit = lax.shift_right_logical(byte, mod(iota((tall, width), 1), 8)) & 1
        flag = bit.astype(jnp.float32).astype(jnp.bfloat16)
        kind[r, :] = jnp.concatenate([fw[r, :]] * (width // 128), axis=1) * flag

        f = b // (steps // FOLDS)
        q = pl.ds(pl.multiple_of(lax.rem(b, steps // FOLDS) * quarter, quarter), quarter)
        left_f = lw[q, pl.ds(pl.multiple_of(f * RANK, RANK), RANK)]
        pred[f, q, :] = dot(left_f, right[f], NT).astype(jnp.bfloat16)
        return carry

    def collect(at):
        swap_recv(*datas[at])
        cols = slice(at * part, (at + 1) * part)

        arrived = got[:, :, cols].reshape(CORE, part)
        dpack[:, cols] = dot(umat[CORE : CORE + PACK, :], arrived).astype(jnp.bfloat16)
        dw[0:CORE, cols] = dot(umat[0:CORE, :], arrived).astype(jnp.bfloat16)
        halo_start(*halos[at])

    def finish(at):
        cols = slice(at * part, (at + 1) * part)
        halo_recv(*halos[at])
        newb = []
        for f in range(FOLDS):
            sort = kind[:, cols]
            train = (sort > 0.5) & (sort != f + 1.0)
            filled = jnp.where(train, dw[:, cols], pred[f, :, cols])
            total = dot(lt[f], filled)
            update = dot(gram[f], total, precision=lax.Precision.HIGHEST)
            cross[f, :, cols] = update
            newb.append(update.astype(jnp.bfloat16))
        chosen = dot(csel[...], jnp.concatenate(newb, axis=0))
        live = kind[0:CORE, cols].astype(jnp.float32) > 0.5
        diff = dw[0:CORE, cols].astype(jnp.float32) - chosen
        resid = jnp.where(live, diff, 0.0).astype(jnp.bfloat16)
        block = dot(vmat[...], resid).astype(jnp.bfloat16)
        back[:, :, cols] = block.reshape(peers, cap, part)
        ret[me, :, cols] = back[me, :, cols]
        swap_start(*rets[at])

    def deliver(at):
        cols = slice(at * part, (at + 1) * part)
        swap_recv(*rets[at])
        out[:, cols] = dot(qmat[...], ret[:, :, cols].reshape(CORE, part)).astype(jnp.bfloat16)

    lax.fori_loop(0, steps // 2, eliminate, 0)
    collect(0)
    lax.fori_loop(steps // 2, steps, eliminate, 0)
    collect(1)
    for at in range(PARTS):
        finish(at)
        if at + 2 < PARTS:
            collect(at + 2)

    for f in range(FOLDS):
        news[f] = cross[f].T

    for at in range(PARTS):
        deliver(at)

    swap_sent(*metas)
    halo_sent(*lefts)
    halo_sent(*folds)
    for at in range(PARTS):
        swap_sent(*datas[at])
        swap_sent(*rets[at])
        halo_sent(*halos[at])


def fused(acq_traces, route_owner, route_row, route_fold, sample_bits, left_factors, right_factors):
    n_long = lax.axis_size("mlong")
    n_short = lax.axis_size("mshort")
    peers = n_long * n_short
    rows, width = acq_traces.shape
    cap = rows // peers
    low = jnp.bitwise_and(sample_bits, 255).astype(jnp.bfloat16)
    high = lax.shift_right_logical(sample_bits, 8).astype(jnp.bfloat16)
    side = jnp.concatenate([left_factors.reshape(rows, WIDE), low, high], axis=1)
    vmem = pl.BlockSpec(memory_space=pltpu.VMEM)
    bf = jnp.bfloat16
    dma = pltpu.SemaphoreType.DMA
    return pl.pallas_call(
        functools.partial(kernel, n_long, n_short),
        out_shape=(
            jax.ShapeDtypeStruct((FOLDS, width, RANK), jnp.float32),
            jax.ShapeDtypeStruct((rows, width), bf),
        ),
        in_specs=[vmem] * 6,
        out_specs=(vmem, vmem),
        scratch_shapes=[
            pltpu.VMEM((WIN, WIDE + 128), bf),
            pltpu.VMEM((PACK, WIDE + 128), bf),
            pltpu.VMEM((WIN, 128), bf),
            pltpu.VMEM((PACK, 128), bf),
            pltpu.VMEM((WIN, width), bf),
            pltpu.VMEM((PACK, width), bf),
            pltpu.VMEM((peers, 1, 128), jnp.float32),
            pltpu.VMEM((peers, 1, 128), jnp.float32),
            pltpu.VMEM((peers, cap, width), bf),
            pltpu.VMEM((peers, cap, width), bf),
            pltpu.VMEM((peers, cap, width), bf),
            pltpu.VMEM((peers, cap, width), bf),
            pltpu.VMEM((FOLDS, WIN, width), bf),
            pltpu.VMEM((WIN, width), bf),
            pltpu.VMEM((FOLDS, RANK, width), jnp.float32),
            pltpu.VMEM((FOLDS, RANK, WIN), bf),
            pltpu.VMEM((FOLDS, RANK, RANK), jnp.float32),
            pltpu.VMEM((CORE + PACK, CORE), bf),
            pltpu.VMEM((CORE, CORE), bf),
            pltpu.VMEM((CORE, CORE), bf),
            pltpu.VMEM((CORE, WIDE), bf),
            dma((1,)), dma((1,)), dma((PARTS,)), dma((PARTS,)), dma((PARTS,)), dma((PARTS,)),
            dma((1, 8)), dma((1, 8)), dma((1, 8)), dma((1, 8)), dma((PARTS, 8)), dma((PARTS, 8)),
        ],
        compiler_params=pltpu.CompilerParams(
            collective_id=0, has_side_effects=True, vmem_limit_bytes=44 * 1024 * 1024
        ),
    )(
        acq_traces, route_owner.reshape(1, rows), route_row.reshape(1, rows), route_fold.reshape(1, rows),
        side, right_factors,
    )


def solution(mesh):
    in_specs = (
        P(("mlong", "mshort"), None),
        P(("mlong", "mshort")),
        P(("mlong", "mshort")),
        P(("mlong", "mshort")),
        P(("mlong", "mshort"), None),
        P(("mlong", "mshort"), None, None),
        P(None, ("mlong", "mshort"), None),
    )
    out_specs = (P(None, ("mlong", "mshort"), None), P(("mlong", "mshort"), None))
    peers = mesh.shape["mlong"] * mesh.shape["mshort"]
    body = fused if peers * 16 == CX * CY else local
    return jax.shard_map(body, mesh=mesh, in_specs=in_specs, out_specs=out_specs, check_vma=False)
```

```python
import functools

import jax
import jax.numpy as jnp
from jax import lax
from jax.experimental import pallas as pl
from jax.experimental.pallas import tpu as pltpu
from jax.sharding import PartitionSpec as P

RANK = 128
FOLDS = 4
H = 4
CX = 16
CY = 32


def padded(x, sides, width):
    for axis, dim in sides:
        count, length = (lax.axis_size(axis), x.shape[dim])
        up = [(i, (i + 1) % count) for i in range(count - 1)]
        down = [(j, i) for i, j in up]
        last = lax.slice_in_dim(x, length - width, length, axis=dim)
        initial = lax.slice_in_dim(x, 0, width, axis=dim)
        before = lax.ppermute(last, axis, up)
        after = lax.ppermute(initial, axis, down)
        x = jnp.concatenate([before, x, after], axis=dim)
    return x


def unpack(bits):
    shifts = jnp.arange(16, dtype=jnp.int32)
    flags = jnp.bitwise_and(lax.shift_right_logical(bits[:, :, None], shifts[None, None, :]), 1)
    return flags.reshape(bits.shape[0], -1).astype(jnp.float32)


def chol_right(cross, gram):
    chol = jnp.linalg.cholesky(gram)
    first = lax.linalg.triangular_solve(chol, cross, left_side=False, lower=True, transpose_a=True)
    return lax.linalg.triangular_solve(chol, first, left_side=False, lower=True, transpose_a=False)


def local(acq_traces, route_owner, route_row, route_fold, sample_bits, left_factors, right_factors):
    n_long = lax.axis_size("mlong")
    n_short = lax.axis_size("mshort")
    peers = n_long * n_short
    rows = acq_traces.shape[0]
    width = acq_traces.shape[1]
    cap = rows // peers
    total = peers * cap
    grid_bits = sample_bits.reshape(CX, CY, width // 16)
    grid_left = left_factors.reshape(CX, CY, FOLDS * RANK)
    valid = route_owner >= 0
    owner = jnp.where(valid, route_owner, 0)
    onehot = (
        (owner[:, None] == jnp.arange(peers, dtype=jnp.int32)[None, :]) & valid[:, None]
    ).astype(jnp.int32)
    within = jnp.sum(jnp.cumsum(onehot, axis=0) * onehot, axis=1) - 1
    place = jnp.where(valid, owner * cap + within, total)
    source = (
        jnp.full((total,), rows, jnp.int32)
        .at[place]
        .set(jnp.arange(rows, dtype=jnp.int32), mode="drop")
    )
    filled_slot = source < rows
    pick = jnp.minimum(source, rows - 1)
    send_traces = jnp.where(
        filled_slot[:, None], jnp.take(acq_traces, pick, axis=0), jnp.zeros((), jnp.bfloat16)
    )
    send_rows = jnp.where(filled_slot, jnp.take(route_row, pick), -1)
    send_folds = jnp.where(filled_slot, jnp.take(route_fold, pick), -1)
    got_traces, got_rows, got_folds = (
        lax.all_to_all(send_traces, ("mlong", "mshort"), split_axis=0, concat_axis=0, tiled=True),
        lax.all_to_all(send_rows, ("mlong", "mshort"), split_axis=0, concat_axis=0, tiled=True),
        lax.all_to_all(send_folds, ("mlong", "mshort"), split_axis=0, concat_axis=0, tiled=True),
    )
    arrival = (
        jnp.full((rows,), total, jnp.int32)
        .at[jnp.where(got_rows >= 0, got_rows, rows)]
        .set(jnp.arange(total, dtype=jnp.int32), mode="drop")
    )
    present = arrival < total
    slot_at = jnp.minimum(arrival, total - 1)
    data = jnp.where(
        present[:, None], jnp.take(got_traces, slot_at, axis=0), jnp.zeros((), jnp.bfloat16)
    )
    fold = jnp.where(present, jnp.take(got_folds, slot_at), -1)
    wide_data, wide_bits, wide_fold, wide_left = (
        padded(data.reshape(CX, CY, width), (("mlong", 0), ("mshort", 1)), H),
        padded(grid_bits, (("mlong", 0), ("mshort", 1)), H),
        padded(fold.reshape(CX, CY), (("mlong", 0), ("mshort", 1)), H),
        padded(grid_left, (("mlong", 0), ("mshort", 1)), H),
    )
    d_win = wide_data.reshape(-1, width)
    f_win = wide_fold.reshape(-1)
    l_win = wide_left.reshape(-1, FOLDS, RANK)
    seen = unpack(wide_bits.reshape(-1, width // 16)) * (f_win >= 0)[:, None].astype(jnp.float32)
    s_core = unpack(sample_bits) * (fold >= 0)[:, None].astype(jnp.float32)
    ridge = jnp.eye(RANK, dtype=jnp.float32)
    updates = []
    chosen = jnp.zeros((rows, width), jnp.float32)
    for f in range(FOLDS):
        factor = l_win[:, f]
        pred = jnp.dot(factor, right_factors[f].T, preferred_element_type=jnp.float32)
        train = seen * (f_win != f)[:, None].astype(jnp.float32)
        imputed = (train * d_win.astype(jnp.float32) + (1.0 - train) * pred).astype(jnp.bfloat16)
        cross = jnp.dot(imputed.T, factor, preferred_element_type=jnp.float32)
        gram = jnp.dot(factor.T, factor, preferred_element_type=jnp.float32) + ridge
        update = chol_right(cross, gram)
        updates.append(update)
        core_pred = jnp.dot(
            left_factors[:, f], update.astype(jnp.bfloat16).T, preferred_element_type=jnp.float32
        )
        chosen = chosen + (fold == f)[:, None].astype(jnp.float32) * core_pred
    new_right = jnp.stack(updates)
    resid = (s_core * (data.astype(jnp.float32) - chosen)).astype(jnp.bfloat16)
    back = jnp.where(
        (got_rows >= 0)[:, None],
        jnp.take(resid, jnp.maximum(got_rows, 0), axis=0),
        jnp.zeros((), jnp.bfloat16),
    )
    returned = lax.all_to_all(back, ("mlong", "mshort"), split_axis=0, concat_axis=0, tiled=True)
    trace_residuals = jnp.where(
        valid[:, None],
        jnp.take(returned, jnp.minimum(place, total - 1), axis=0),
        jnp.zeros((), jnp.bfloat16),
    )
    return (new_right, trace_residuals)


MESH = pl.DeviceIdType.MESH
WIN = 1024
CORE = CX * CY
WIDE = FOLDS * RANK
PARTS = 2
NT = (((1,), (1,)), ((), ()))
HALO = (
    (1, 0, False, CORE - H * CY, CORE, H * CY),
    (-1, 0, False, 0, CORE + H * CY, H * CY),
    (0, 1, True, H * CX, CORE + 2 * H * CY, H * CX),
    (0, -1, True, 0, CORE + 2 * H * CY + H * CX, H * CX),
    (1, 1, True, 2 * H * CX + 48, CORE + 2 * H * (CX + CY), 16),
    (1, -1, True, 2 * H * CX + 32, CORE + 2 * H * (CX + CY) + 16, 16),
    (-1, 1, True, 2 * H * CX + 16, CORE + 2 * H * (CX + CY) + 32, 16),
    (-1, -1, True, 2 * H * CX, CORE + 2 * H * (CX + CY) + 48, 16),
)
PACK = 2 * H * CX + 64


def iota(shape, dim):
    return lax.broadcasted_iota(jnp.int32, shape, dim)


def flags(mask, dtype=jnp.bfloat16):
    return jnp.where(mask, 1.0, 0.0).astype(dtype)


def dot(a, b, dims=(((1,), (0,)), ((), ())), precision=None):
    return lax.dot_general(a, b, dims, precision=precision, preferred_element_type=jnp.float32)


def div(x, n):
    return lax.shift_right_arithmetic(x, n.bit_length() - 1)


def mod(x, n):
    return x & (n - 1)


def packed_rows(shape):
    t = iota(shape, 0)
    u = t - 2 * H * CX
    v = mod(t, H * CX)
    edge = div(v, H) * CY + mod(v, H) + jnp.where(t < H * CX, 0, CY - H)
    k = div(u, 16)
    w = mod(u, 16)
    corner = (div(w, H) + jnp.where(k >= 2, CX - H, 0)) * CY + mod(w, H) + jnp.where(mod(k, 2) == 1, CY - H, 0)
    return jnp.where(u < 0, edge, corner)


def pieces(x):
    top = x.astype(jnp.bfloat16).astype(jnp.float32)
    rest = x - top
    middle = rest.astype(jnp.bfloat16).astype(jnp.float32)
    return top, middle, rest - middle


def kernel(
    n_long, n_short, traces, own, row, fold, side, right, news, out,
    lw, lpack, fw, fpack, dw, dpack, meta_out, meta_in, send, got, ret, back, kind, cross, lt, ltm, gram, umat, vmat, qmat, csel,
    meta_s, meta_r, data_s, data_r, ret_s, ret_r, hl_s, hl_r, hf_s, hf_r, hd_s, hd_r,
):
    peers = n_long * n_short
    cap = CORE // peers
    a = lax.axis_index("mlong")
    c = lax.axis_index("mshort")
    me = a * n_short + c
    width = traces.shape[1]

    lw[0:CORE, :] = side[...]
    lw[CORE:WIN, :] = jnp.zeros((WIN - CORE, WIDE + 128), jnp.bfloat16)
    fw[CORE:WIN, :] = jnp.zeros((WIN - CORE, 128), jnp.bfloat16)
    dw[CORE:WIN, :] = jnp.zeros((WIN - CORE, width), jnp.bfloat16)
    part = width // PARTS

    barrier = pltpu.get_barrier_semaphore()

    others = [None]
    for k in range(1, peers):
        q = lax.rem(me + k, peers)
        others.append((q, (q // n_short, lax.rem(q, n_short))))
        pl.semaphore_signal(barrier, inc=1, device_id=others[k][1], device_id_type=MESH)

    owner = own[...]
    oh = flags(iota((peers, CORE), 0) == owner, jnp.float32)
    tri = flags(iota((CORE, CORE), 0) < iota((CORE, CORE), 1))
    cum = dot(oh.astype(jnp.bfloat16), tri)
    within = jnp.sum(oh * cum, axis=0, keepdims=True).astype(jnp.int32)
    place = jnp.where(owner >= 0, owner * cap + within, -1)
    rows = row[...]
    vals = [div(rows, 128).astype(jnp.float32), mod(rows, 128).astype(jnp.float32), (fold[...] + 1).astype(jnp.float32)]
    left = jnp.concatenate([oh * v for v in vals], axis=1).astype(jnp.bfloat16)
    rightm = jnp.concatenate([flags(iota((128, CORE), 0) == within + 32 * i) for i in range(3)], axis=1)
    meta = dot(left, rightm, NT)
    for p in range(peers):
        meta_out[p] = meta[p : p + 1, :]
    meta_in[me] = meta_out[me]

    pl.semaphore_wait(barrier, peers - 1)

    def halo(buffer, pack, send_sem, recv_sem, at, span, i):
        da, dc, packed, start, dst, count = HALO[i]
        here = pack if packed else buffer
        return pltpu.make_async_remote_copy(
            src_ref=here.at[pl.ds(start, count), pl.ds(at * span, span)],
            dst_ref=buffer.at[pl.ds(dst, count), pl.ds(at * span, span)],
            send_sem=send_sem.at[at, i],
            recv_sem=recv_sem.at[at, i],
            device_id=(a + da, c + dc),
            device_id_type=MESH,
        )

    def inside(da, dc):
        return (a + da >= 0) & (a + da < n_long) & (c + dc >= 0) & (c + dc < n_short)

    def halo_start(*refs):
        for i in range(8):
            @pl.when(inside(HALO[i][0], HALO[i][1]))
            def _():
                halo(*refs, i).start()

    def halo_recv(*refs):
        for i in range(8):
            @pl.when(inside(-HALO[i][0], -HALO[i][1]))
            def _():
                halo(*refs, i).wait_recv()

    def halo_sent(*refs):
        for i in range(8):
            @pl.when(inside(HALO[i][0], HALO[i][1]))
            def _():
                halo(*refs, i).wait_send()

    def swap(src, dst, send_sem, recv_sem, at, span, k):
        to, place_of_to = others[k]
        return pltpu.make_async_remote_copy(
            src_ref=src.at[to, :, pl.ds(at * span, span)],
            dst_ref=dst.at[me, :, pl.ds(at * span, span)],
            send_sem=send_sem.at[at],
            recv_sem=recv_sem.at[at],
            device_id=place_of_to,
            device_id_type=MESH,
        )

    def all_of(src, dst, send_sem, recv_sem, at, span):
        return pltpu.make_async_remote_copy(
            src_ref=src.at[pl.ds(1, peers - 1), :, pl.ds(at * span, span)],
            dst_ref=dst.at[pl.ds(1, peers - 1), :, pl.ds(at * span, span)],
            send_sem=send_sem.at[at],
            recv_sem=recv_sem.at[at],
            device_id=(a, lax.rem(c + 1, n_short)),
            device_id_type=MESH,
        )

    def swap_start(*refs):
        for k in range(1, peers):
            swap(*refs, k).start()

    def swap_recv(*refs):
        all_of(*refs).wait_recv()

    def swap_sent(*refs):
        all_of(*refs).wait_send()

    metas = (meta_out, meta_in, meta_s, meta_r, 0, 128)
    datas = [(send, got, data_s, data_r, at, part) for at in range(PARTS)]
    rets = [(back, ret, ret_s, ret_r, at, part) for at in range(PARTS)]
    lefts = (lw, lpack, hl_s, hl_r, 0, WIDE + 128)
    folds = (fw, fpack, hf_s, hf_r, 0, 128)
    halos = [(dw, dpack, hd_s, hd_r, at, part) for at in range(PARTS)]
    swap_start(*metas)

    take = flags(iota((CORE, CORE), 0) == place)
    for at in range(PARTS):
        cols = slice(at * part, (at + 1) * part)
        send[:, :, cols] = dot(take, traces[:, cols]).astype(jnp.bfloat16).reshape(peers, cap, part)
        swap_start(*datas[at])
    got[me] = send[me]

    pick = flags(packed_rows((PACK, CORE)) == iota((PACK, CORE), 1))
    lpack[...] = dot(pick, side[...]).astype(jnp.bfloat16)
    halo_start(*lefts)

    eye = iota((CORE, CORE), 0) == iota((CORE, CORE), 1)

    def column(line):
        return jnp.sum(jnp.where(eye, line.astype(jnp.float32), 0.0), axis=1, keepdims=True).astype(jnp.int32)

    qmat[...] = flags(column(place) == iota((CORE, CORE), 1))

    swap_recv(*metas)
    meta_got = meta_in[:, 0, :].astype(jnp.bfloat16)
    mine = iota((peers, CORE), 0) == div(iota((peers, CORE), 1), cap)
    lines = []
    for i in range(3):
        place_of = flags(iota((128, CORE), 0) == mod(iota((128, CORE), 1), cap) + 32 * i)
        lines.append(jnp.sum(jnp.where(mine, dot(meta_got, place_of), 0.0), axis=0, keepdims=True))
    got_row = jnp.where(lines[2] > 0.5, lines[0] * 128.0 + lines[1], -1.0).astype(jnp.int32)
    got_fold = jnp.broadcast_to(lines[2], (128, CORE)).astype(jnp.bfloat16)
    umat[...] = flags(iota((CORE, CORE), 0) == got_row)
    fw[0:CORE, :] = dot(umat[...], got_fold, NT).astype(jnp.bfloat16)
    fpack[...] = dot(pick, fw[0:CORE, :]).astype(jnp.bfloat16)
    halo_start(*folds)
    vmat[...] = flags(column(got_row) == iota((CORE, CORE), 1))
    for f in range(FOLDS):
        fs = slice(f * RANK, (f + 1) * RANK)
        csel[:, fs] = jnp.where(fw[0:CORE, :] == f + 1.0, side[:, fs], jnp.zeros((CORE, RANK), jnp.bfloat16))

    halo_recv(*lefts)
    for f in range(FOLDS):
        factor = lw[:, f * RANK : (f + 1) * RANK]
        lt[f] = factor.T
        ident = flags(iota((RANK, RANK), 0) == iota((RANK, RANK), 1), jnp.float32)
        gram[f] = dot(lt[f], factor) + ident

    halo_recv(*folds)
    words = iota((128, width), 0)
    offs = iota((128, width), 1)
    expand = flags(words == div(offs, 16) + jnp.where(mod(offs, 16) >= 8, 64, 0))
    steps = RANK // 8
    tall = WIN // steps

    cross[...] = jnp.zeros_like(cross)
    sorts = fw[...].astype(jnp.float32)
    for f in range(FOLDS):
        kept = jnp.where((sorts > 0.5) & (sorts != f + 1.0), lw[:, f * RANK : (f + 1) * RANK].astype(jnp.float32), 0.0)
        ltm[f * RANK : (f + 1) * RANK, :] = kept.astype(jnp.bfloat16).T

    def classify(start, count):
        r = pl.ds(start, count)
        byte = dot(lw[r, WIDE : WIDE + 128], expand).astype(jnp.int32)
        bit = lax.shift_right_logical(byte, mod(iota((count, width), 1), 8)) & 1
        flag = bit.astype(jnp.float32).astype(jnp.bfloat16)
        kind[r, :] = jnp.concatenate([fw[r, :]] * (width // 128), axis=1) * flag

    quarter = WIN // FOLDS
    classify(0, quarter)

    def eliminate(b, carry):
        k0 = pl.multiple_of(b * 8, 8)
        first = gram[:, pl.ds(k0, 8), :]
        lane = iota((FOLDS, 8, RANK), 2)
        sub = iota((FOLDS, 8, RANK), 1)
        inner = (lane >= k0) & (lane < k0 + 8)
        cols = [
            jnp.broadcast_to(jnp.sum(jnp.where(lane == k0 + j, first, 0.0), axis=2, keepdims=True), first.shape)
            for j in range(8)
        ]
        panel = jnp.where(inner, jnp.where(lane - k0 == sub, 1.0, 0.0), first)
        for j in range(8):
            pivot = cols[j]
            inv = 1.0 / pivot[:, j : j + 1, :]

            def reduce_rows(x):
                w = x[:, j : j + 1, :] * inv
                return jnp.where(sub == j, w, x - pivot * w)

            panel = reduce_rows(panel)
            cols = [reduce_rows(x) if i > j else x for i, x in enumerate(cols)]
        signed = jnp.where(lane < k0, -first, first)
        keep = (iota((RANK, RANK), 1) < k0) | (iota((RANK, RANK), 1) >= k0 + 8)
        for f in range(FOLDS):
            a1, a2, a3 = pieces(signed[f])
            b1, b2, b3 = pieces(panel[f])
            lhs = jnp.concatenate([a1, a1, a2, a2, a1, a3, jnp.zeros((80, RANK), jnp.float32)], axis=0).T
            rhs = jnp.concatenate([b1, b2, b1, b2, b3, b1, jnp.zeros((80, RANK), jnp.float32)], axis=0)
            change = dot(lhs.astype(jnp.bfloat16), rhs.astype(jnp.bfloat16))
            gram[f] = jnp.where(keep, gram[f], 0.0) - change
        gram[:, pl.ds(k0, 8), :] = panel

        f = lax.rem(b, FOLDS)
        q = pl.multiple_of(b // FOLDS * quarter, quarter)
        r = pl.ds(q, quarter)
        sort = kind[r, :]
        left_f = lw[r, pl.ds(pl.multiple_of(f * RANK, RANK), RANK)]
        guess = dot(left_f, right[f], NT).astype(jnp.bfloat16)
        train = (sort > 0.5) & (sort != (f + 1).astype(jnp.bfloat16))
        missing = jnp.where(train, jnp.zeros_like(guess), guess)
        cross[f] += dot(lt[f, :, r], missing)
        classify(pl.multiple_of(lax.rem(b + FOLDS, steps) * tall, tall), tall)
        return carry

    def collect(at):
        swap_recv(*datas[at])
        cols = slice(at * part, (at + 1) * part)

        arrived = got[:, :, cols].reshape(CORE, part)
        present = kind[0:CORE, cols].astype(jnp.float32) > 0.5
        dw[0:CORE, cols] = jnp.where(present, dot(umat[...], arrived), 0.0).astype(jnp.bfloat16)
        dpack[:, cols] = dot(pick, dw[0:CORE, cols]).astype(jnp.bfloat16)
        halo_start(*halos[at])

    def finish(at):
        cols = slice(at * part, (at + 1) * part)
        halo_recv(*halos[at])
        known = dot(ltm[...], dw[:, cols])
        newb = []
        for f in range(FOLDS):
            total = known[f * RANK : (f + 1) * RANK, :] + cross[f, :, cols]
            a1, a2, a3 = pieces(gram[f])
            b1, b2, b3 = pieces(total)
            lhs = jnp.concatenate([a1, a1, a2, a2, a1, a3], axis=1).astype(jnp.bfloat16)
            rhs = jnp.concatenate([b1, b2, b1, b2, b3, b1], axis=0).astype(jnp.bfloat16)
            update = dot(lhs, rhs)
            cross[f, :, cols] = update
            newb.append(update.astype(jnp.bfloat16))
        chosen = dot(csel[...], jnp.concatenate(newb, axis=0))
        live = kind[0:CORE, cols].astype(jnp.float32) > 0.5
        diff = dw[0:CORE, cols].astype(jnp.float32) - chosen
        resid = jnp.where(live, diff, 0.0).astype(jnp.bfloat16)
        block = dot(vmat[...], resid).astype(jnp.bfloat16)
        back[:, :, cols] = block.reshape(peers, cap, part)
        ret[me, :, cols] = back[me, :, cols]
        swap_start(*rets[at])

    def deliver(at):
        cols = slice(at * part, (at + 1) * part)
        swap_recv(*rets[at])
        out[:, cols] = dot(qmat[...], ret[:, :, cols].reshape(CORE, part)).astype(jnp.bfloat16)

    lax.fori_loop(0, steps // 2, eliminate, 0)
    collect(0)
    lax.fori_loop(steps // 2, steps, eliminate, 0)
    collect(1)
    for at in range(PARTS):
        finish(at)
        if at + 2 < PARTS:
            collect(at + 2)

    for f in range(FOLDS):
        news[f] = cross[f].T

    for at in range(PARTS):
        deliver(at)

    swap_sent(*metas)
    halo_sent(*lefts)
    halo_sent(*folds)
    for at in range(PARTS):
        swap_sent(*datas[at])
        swap_sent(*rets[at])
        halo_sent(*halos[at])


def fused(acq_traces, route_owner, route_row, route_fold, sample_bits, left_factors, right_factors):
    n_long = lax.axis_size("mlong")
    n_short = lax.axis_size("mshort")
    peers = n_long * n_short
    rows, width = acq_traces.shape
    cap = rows // peers
    low = jnp.bitwise_and(sample_bits, 255).astype(jnp.bfloat16)
    high = lax.shift_right_logical(sample_bits, 8).astype(jnp.bfloat16)
    side = jnp.concatenate([left_factors.reshape(rows, WIDE), low, high], axis=1)
    vmem = pl.BlockSpec(memory_space=pltpu.VMEM)
    bf = jnp.bfloat16
    dma = pltpu.SemaphoreType.DMA
    return pl.pallas_call(
        functools.partial(kernel, n_long, n_short),
        out_shape=(
            jax.ShapeDtypeStruct((FOLDS, width, RANK), jnp.float32),
            jax.ShapeDtypeStruct((rows, width), bf),
        ),
        in_specs=[vmem] * 6,
        out_specs=(vmem, vmem),
        scratch_shapes=[
            pltpu.VMEM((WIN, WIDE + 128), bf),
            pltpu.VMEM((PACK, WIDE + 128), bf),
            pltpu.VMEM((WIN, 128), bf),
            pltpu.VMEM((PACK, 128), bf),
            pltpu.VMEM((WIN, width), bf),
            pltpu.VMEM((PACK, width), bf),
            pltpu.VMEM((peers, 1, 128), jnp.float32),
            pltpu.VMEM((peers, 1, 128), jnp.float32),
            pltpu.VMEM((peers, cap, width), bf),
            pltpu.VMEM((peers, cap, width), bf),
            pltpu.VMEM((peers, cap, width), bf),
            pltpu.VMEM((peers, cap, width), bf),
            pltpu.VMEM((WIN, width), bf),
            pltpu.VMEM((FOLDS, RANK, width), jnp.float32),
            pltpu.VMEM((FOLDS, RANK, WIN), bf),
            pltpu.VMEM((WIDE, WIN), bf),
            pltpu.VMEM((FOLDS, RANK, RANK), jnp.float32),
            pltpu.VMEM((CORE, CORE), bf),
            pltpu.VMEM((CORE, CORE), bf),
            pltpu.VMEM((CORE, CORE), bf),
            pltpu.VMEM((CORE, WIDE), bf),
            dma((1,)), dma((1,)), dma((PARTS,)), dma((PARTS,)), dma((PARTS,)), dma((PARTS,)),
            dma((1, 8)), dma((1, 8)), dma((1, 8)), dma((1, 8)), dma((PARTS, 8)), dma((PARTS, 8)),
        ],
        compiler_params=pltpu.CompilerParams(
            collective_id=0, has_side_effects=True, vmem_limit_bytes=40 * 1024 * 1024
        ),
    )(
        acq_traces, route_owner.reshape(1, rows), route_row.reshape(1, rows), route_fold.reshape(1, rows),
        side, right_factors,
    )


def solution(mesh):
    in_specs = (
        P(("mlong", "mshort"), None),
        P(("mlong", "mshort")),
        P(("mlong", "mshort")),
        P(("mlong", "mshort")),
        P(("mlong", "mshort"), None),
        P(("mlong", "mshort"), None, None),
        P(None, ("mlong", "mshort"), None),
    )
    out_specs = (P(None, ("mlong", "mshort"), None), P(("mlong", "mshort"), None))
    peers = mesh.shape["mlong"] * mesh.shape["mshort"]
    body = fused if peers * 16 == CX * CY else local
    return jax.shard_map(body, mesh=mesh, in_specs=in_specs, out_specs=out_specs, check_vma=False)
```

```python
import functools

import jax
import jax.numpy as jnp
from jax import lax
from jax.experimental import pallas as pl
from jax.experimental.pallas import tpu as pltpu
from jax.sharding import PartitionSpec as P

RANK = 128
FOLDS = 4
H = 4
CX = 16
CY = 32


def padded(x, sides, width):
    for axis, dim in sides:
        count, length = (lax.axis_size(axis), x.shape[dim])
        up = [(i, (i + 1) % count) for i in range(count - 1)]
        down = [(j, i) for i, j in up]
        last = lax.slice_in_dim(x, length - width, length, axis=dim)
        initial = lax.slice_in_dim(x, 0, width, axis=dim)
        before = lax.ppermute(last, axis, up)
        after = lax.ppermute(initial, axis, down)
        x = jnp.concatenate([before, x, after], axis=dim)
    return x


def unpack(bits):
    shifts = jnp.arange(16, dtype=jnp.int32)
    flags = jnp.bitwise_and(lax.shift_right_logical(bits[:, :, None], shifts[None, None, :]), 1)
    return flags.reshape(bits.shape[0], -1).astype(jnp.float32)


def chol_right(cross, gram):
    chol = jnp.linalg.cholesky(gram)
    first = lax.linalg.triangular_solve(chol, cross, left_side=False, lower=True, transpose_a=True)
    return lax.linalg.triangular_solve(chol, first, left_side=False, lower=True, transpose_a=False)


def local(acq_traces, route_owner, route_row, route_fold, sample_bits, left_factors, right_factors):
    n_long = lax.axis_size("mlong")
    n_short = lax.axis_size("mshort")
    peers = n_long * n_short
    rows = acq_traces.shape[0]
    width = acq_traces.shape[1]
    cap = rows // peers
    total = peers * cap
    grid_bits = sample_bits.reshape(CX, CY, width // 16)
    grid_left = left_factors.reshape(CX, CY, FOLDS * RANK)
    valid = route_owner >= 0
    owner = jnp.where(valid, route_owner, 0)
    onehot = (
        (owner[:, None] == jnp.arange(peers, dtype=jnp.int32)[None, :]) & valid[:, None]
    ).astype(jnp.int32)
    within = jnp.sum(jnp.cumsum(onehot, axis=0) * onehot, axis=1) - 1
    place = jnp.where(valid, owner * cap + within, total)
    source = (
        jnp.full((total,), rows, jnp.int32)
        .at[place]
        .set(jnp.arange(rows, dtype=jnp.int32), mode="drop")
    )
    filled_slot = source < rows
    pick = jnp.minimum(source, rows - 1)
    send_traces = jnp.where(
        filled_slot[:, None], jnp.take(acq_traces, pick, axis=0), jnp.zeros((), jnp.bfloat16)
    )
    send_rows = jnp.where(filled_slot, jnp.take(route_row, pick), -1)
    send_folds = jnp.where(filled_slot, jnp.take(route_fold, pick), -1)
    got_traces, got_rows, got_folds = (
        lax.all_to_all(send_traces, ("mlong", "mshort"), split_axis=0, concat_axis=0, tiled=True),
        lax.all_to_all(send_rows, ("mlong", "mshort"), split_axis=0, concat_axis=0, tiled=True),
        lax.all_to_all(send_folds, ("mlong", "mshort"), split_axis=0, concat_axis=0, tiled=True),
    )
    arrival = (
        jnp.full((rows,), total, jnp.int32)
        .at[jnp.where(got_rows >= 0, got_rows, rows)]
        .set(jnp.arange(total, dtype=jnp.int32), mode="drop")
    )
    present = arrival < total
    slot_at = jnp.minimum(arrival, total - 1)
    data = jnp.where(
        present[:, None], jnp.take(got_traces, slot_at, axis=0), jnp.zeros((), jnp.bfloat16)
    )
    fold = jnp.where(present, jnp.take(got_folds, slot_at), -1)
    wide_data, wide_bits, wide_fold, wide_left = (
        padded(data.reshape(CX, CY, width), (("mlong", 0), ("mshort", 1)), H),
        padded(grid_bits, (("mlong", 0), ("mshort", 1)), H),
        padded(fold.reshape(CX, CY), (("mlong", 0), ("mshort", 1)), H),
        padded(grid_left, (("mlong", 0), ("mshort", 1)), H),
    )
    d_win = wide_data.reshape(-1, width)
    f_win = wide_fold.reshape(-1)
    l_win = wide_left.reshape(-1, FOLDS, RANK)
    seen = unpack(wide_bits.reshape(-1, width // 16)) * (f_win >= 0)[:, None].astype(jnp.float32)
    s_core = unpack(sample_bits) * (fold >= 0)[:, None].astype(jnp.float32)
    ridge = jnp.eye(RANK, dtype=jnp.float32)
    updates = []
    chosen = jnp.zeros((rows, width), jnp.float32)
    for f in range(FOLDS):
        factor = l_win[:, f]
        pred = jnp.dot(factor, right_factors[f].T, preferred_element_type=jnp.float32)
        train = seen * (f_win != f)[:, None].astype(jnp.float32)
        imputed = (train * d_win.astype(jnp.float32) + (1.0 - train) * pred).astype(jnp.bfloat16)
        cross = jnp.dot(imputed.T, factor, preferred_element_type=jnp.float32)
        gram = jnp.dot(factor.T, factor, preferred_element_type=jnp.float32) + ridge
        update = chol_right(cross, gram)
        updates.append(update)
        core_pred = jnp.dot(
            left_factors[:, f], update.astype(jnp.bfloat16).T, preferred_element_type=jnp.float32
        )
        chosen = chosen + (fold == f)[:, None].astype(jnp.float32) * core_pred
    new_right = jnp.stack(updates)
    resid = (s_core * (data.astype(jnp.float32) - chosen)).astype(jnp.bfloat16)
    back = jnp.where(
        (got_rows >= 0)[:, None],
        jnp.take(resid, jnp.maximum(got_rows, 0), axis=0),
        jnp.zeros((), jnp.bfloat16),
    )
    returned = lax.all_to_all(back, ("mlong", "mshort"), split_axis=0, concat_axis=0, tiled=True)
    trace_residuals = jnp.where(
        valid[:, None],
        jnp.take(returned, jnp.minimum(place, total - 1), axis=0),
        jnp.zeros((), jnp.bfloat16),
    )
    return (new_right, trace_residuals)


MESH = pl.DeviceIdType.MESH
WIN = 1024
CORE = CX * CY
WIDE = FOLDS * RANK
PARTS = 2
NT = (((1,), (1,)), ((), ()))
HALO = (
    (1, 0, False, CORE - H * CY, CORE, H * CY),
    (-1, 0, False, 0, CORE + H * CY, H * CY),
    (0, 1, True, H * CX, CORE + 2 * H * CY, H * CX),
    (0, -1, True, 0, CORE + 2 * H * CY + H * CX, H * CX),
    (1, 1, True, 2 * H * CX + 48, CORE + 2 * H * (CX + CY), 16),
    (1, -1, True, 2 * H * CX + 32, CORE + 2 * H * (CX + CY) + 16, 16),
    (-1, 1, True, 2 * H * CX + 16, CORE + 2 * H * (CX + CY) + 32, 16),
    (-1, -1, True, 2 * H * CX, CORE + 2 * H * (CX + CY) + 48, 16),
)
PACK = 2 * H * CX + 64


def iota(shape, dim):
    return lax.broadcasted_iota(jnp.int32, shape, dim)


def flags(mask, dtype=jnp.bfloat16):
    return jnp.where(mask, 1.0, 0.0).astype(dtype)


def dot(a, b, dims=(((1,), (0,)), ((), ())), precision=None):
    return lax.dot_general(a, b, dims, precision=precision, preferred_element_type=jnp.float32)


def div(x, n):
    return lax.shift_right_arithmetic(x, n.bit_length() - 1)


def mod(x, n):
    return x & (n - 1)


def packed_rows(shape):
    t = iota(shape, 0)
    u = t - 2 * H * CX
    v = mod(t, H * CX)
    edge = div(v, H) * CY + mod(v, H) + jnp.where(t < H * CX, 0, CY - H)
    k = div(u, 16)
    w = mod(u, 16)
    corner = (div(w, H) + jnp.where(k >= 2, CX - H, 0)) * CY + mod(w, H) + jnp.where(mod(k, 2) == 1, CY - H, 0)
    return jnp.where(u < 0, edge, corner)


def pieces(x):
    top = x.astype(jnp.bfloat16).astype(jnp.float32)
    rest = x - top
    middle = rest.astype(jnp.bfloat16).astype(jnp.float32)
    return top, middle, rest - middle


def kernel(
    n_long, n_short, traces, own, row, fold, side, right, news, out,
    lw, lpack, fw, fpack, dw, dpack, meta_out, meta_in, send, got, ret, back, kind, cross, lt, ltm, gram, umat, vmat, qmat, csel, expand,
    meta_s, meta_r, data_s, data_r, ret_s, ret_r, hl_s, hl_r, hf_s, hf_r, hd_s, hd_r,
):
    peers = n_long * n_short
    cap = CORE // peers
    a = lax.axis_index("mlong")
    c = lax.axis_index("mshort")
    me = a * n_short + c
    width = traces.shape[1]

    lw[0:CORE, :] = side[...]
    lw[CORE:WIN, :] = jnp.zeros((WIN - CORE, WIDE + 128), jnp.bfloat16)
    fw[CORE:WIN, :] = jnp.zeros((WIN - CORE, 128), jnp.bfloat16)
    dw[CORE:WIN, :] = jnp.zeros((WIN - CORE, width), jnp.bfloat16)
    part = width // PARTS

    barrier = pltpu.get_barrier_semaphore()

    others = [None]
    for k in range(1, peers):
        q = lax.rem(me + k, peers)
        others.append((q, (q // n_short, lax.rem(q, n_short))))
        pl.semaphore_signal(barrier, inc=1, device_id=others[k][1], device_id_type=MESH)

    owner = own[...]
    oh = flags(iota((peers, CORE), 0) == owner, jnp.float32)
    tri = flags(iota((CORE, CORE), 0) < iota((CORE, CORE), 1))
    cum = dot(oh.astype(jnp.bfloat16), tri)
    within = jnp.sum(oh * cum, axis=0, keepdims=True).astype(jnp.int32)
    place = jnp.where(owner >= 0, owner * cap + within, -1)
    rows = row[...]
    vals = [div(rows, 128).astype(jnp.float32), mod(rows, 128).astype(jnp.float32), (fold[...] + 1).astype(jnp.float32)]
    left = jnp.concatenate([oh * v for v in vals], axis=1).astype(jnp.bfloat16)
    rightm = jnp.concatenate([flags(iota((128, CORE), 0) == within + 32 * i) for i in range(3)], axis=1)
    meta = dot(left, rightm, NT)
    for p in range(peers):
        meta_out[p] = meta[p : p + 1, :]
    meta_in[me] = meta_out[me]

    pl.semaphore_wait(barrier, peers - 1)

    def halo(buffer, pack, send_sem, recv_sem, at, span, i):
        da, dc, packed, start, dst, count = HALO[i]
        here = pack if packed else buffer
        return pltpu.make_async_remote_copy(
            src_ref=here.at[pl.ds(start, count), pl.ds(at * span, span)],
            dst_ref=buffer.at[pl.ds(dst, count), pl.ds(at * span, span)],
            send_sem=send_sem.at[at, i],
            recv_sem=recv_sem.at[at, i],
            device_id=(a + da, c + dc),
            device_id_type=MESH,
        )

    def inside(da, dc):
        return (a + da >= 0) & (a + da < n_long) & (c + dc >= 0) & (c + dc < n_short)

    def halo_start(*refs):
        for i in range(8):
            @pl.when(inside(HALO[i][0], HALO[i][1]))
            def _():
                halo(*refs, i).start()

    def halo_recv(*refs):
        for i in range(8):
            @pl.when(inside(-HALO[i][0], -HALO[i][1]))
            def _():
                halo(*refs, i).wait_recv()

    def halo_sent(*refs):
        for i in range(8):
            @pl.when(inside(HALO[i][0], HALO[i][1]))
            def _():
                halo(*refs, i).wait_send()

    def swap(src, dst, send_sem, recv_sem, at, span, k):
        to, place_of_to = others[k]
        return pltpu.make_async_remote_copy(
            src_ref=src.at[to, :, pl.ds(at * span, span)],
            dst_ref=dst.at[me, :, pl.ds(at * span, span)],
            send_sem=send_sem.at[at],
            recv_sem=recv_sem.at[at],
            device_id=place_of_to,
            device_id_type=MESH,
        )

    def all_of(src, dst, send_sem, recv_sem, at, span):
        return pltpu.make_async_remote_copy(
            src_ref=src.at[pl.ds(1, peers - 1), :, pl.ds(at * span, span)],
            dst_ref=dst.at[pl.ds(1, peers - 1), :, pl.ds(at * span, span)],
            send_sem=send_sem.at[at],
            recv_sem=recv_sem.at[at],
            device_id=(a, lax.rem(c + 1, n_short)),
            device_id_type=MESH,
        )

    def swap_start(*refs):
        for k in range(1, peers):
            swap(*refs, k).start()

    def swap_recv(*refs):
        all_of(*refs).wait_recv()

    def swap_sent(*refs):
        all_of(*refs).wait_send()

    metas = (meta_out, meta_in, meta_s, meta_r, 0, 128)
    datas = [(send, got, data_s, data_r, at, part) for at in range(PARTS)]
    rets = [(back, ret, ret_s, ret_r, at, part) for at in range(PARTS)]
    lefts = (lw, lpack, hl_s, hl_r, 0, WIDE + 128)
    folds = (fw, fpack, hf_s, hf_r, 0, 128)
    halos = [(dw, dpack, hd_s, hd_r, at, part) for at in range(PARTS)]
    swap_start(*metas)

    take = flags(iota((CORE, CORE), 0) == place)
    for at in range(PARTS):
        cols = slice(at * part, (at + 1) * part)
        send[:, :, cols] = dot(take, traces[:, cols]).astype(jnp.bfloat16).reshape(peers, cap, part)
        swap_start(*datas[at])
    got[me] = send[me]

    pick = flags(packed_rows((PACK, CORE)) == iota((PACK, CORE), 1))
    lpack[...] = dot(pick, side[...]).astype(jnp.bfloat16)
    halo_start(*lefts)

    eye = iota((CORE, CORE), 0) == iota((CORE, CORE), 1)

    def column(line):
        return jnp.sum(jnp.where(eye, line.astype(jnp.float32), 0.0), axis=1, keepdims=True).astype(jnp.int32)

    qmat[...] = flags(column(place) == iota((CORE, CORE), 1))

    swap_recv(*metas)
    meta_got = meta_in[:, 0, :].astype(jnp.bfloat16)
    mine = iota((peers, CORE), 0) == div(iota((peers, CORE), 1), cap)
    lines = []
    for i in range(3):
        place_of = flags(iota((128, CORE), 0) == mod(iota((128, CORE), 1), cap) + 32 * i)
        lines.append(jnp.sum(jnp.where(mine, dot(meta_got, place_of), 0.0), axis=0, keepdims=True))
    got_row = jnp.where(lines[2] > 0.5, lines[0] * 128.0 + lines[1], -1.0).astype(jnp.int32)
    got_fold = jnp.broadcast_to(lines[2], (128, CORE)).astype(jnp.bfloat16)
    umat[...] = flags(iota((CORE, CORE), 0) == got_row)
    fw[0:CORE, :] = dot(umat[...], got_fold, NT).astype(jnp.bfloat16)
    fpack[...] = dot(pick, fw[0:CORE, :]).astype(jnp.bfloat16)
    halo_start(*folds)
    vmat[...] = flags(column(got_row) == iota((CORE, CORE), 1))
    for f in range(FOLDS):
        fs = slice(f * RANK, (f + 1) * RANK)
        csel[:, fs] = jnp.where(fw[0:CORE, :] == f + 1.0, side[:, fs], jnp.zeros((CORE, RANK), jnp.bfloat16))

    halo_recv(*lefts)
    for f in range(FOLDS):
        factor = lw[:, f * RANK : (f + 1) * RANK]
        lt[f] = factor.T
        ident = flags(iota((RANK, RANK), 0) == iota((RANK, RANK), 1), jnp.float32)
        gram[f] = dot(lt[f], factor) + ident

    halo_recv(*folds)
    words = iota((128, width), 0)
    offs = iota((128, width), 1)
    expand[...] = flags(words == div(offs, 16) + jnp.where(mod(offs, 16) >= 8, 64, 0))
    steps = RANK // 8

    sorts = fw[...].T.astype(jnp.float32)
    for f in range(FOLDS):
        kept = jnp.where((sorts > 0.5) & (sorts != f + 1.0), lt[f].astype(jnp.float32), 0.0)
        ltm[f * RANK : (f + 1) * RANK, :] = kept.astype(jnp.bfloat16)

    tall = WIN // FOLDS
    quarter = width // FOLDS
    shifts = mod(iota((tall, quarter), 1), 8)

    def classify(start, q):
        r = pl.ds(start, tall)
        cols = pl.ds(q, quarter)
        byte = dot(lw[r, WIDE : WIDE + 128], expand[:, cols]).astype(jnp.int32)
        flag = (lax.shift_right_logical(byte, shifts) & 1).astype(jnp.float32).astype(jnp.bfloat16)
        kind[r, cols] = jnp.concatenate([fw[r, :]] * (quarter // 128), axis=1) * flag

    for i in range(FOLDS):
        classify(i * tall, 0)

    def eliminate(b, carry):
        k0 = pl.multiple_of(b * 8, 8)
        first = gram[:, pl.ds(k0, 8), :]
        lane = iota((FOLDS, 8, RANK), 2)
        sub = iota((FOLDS, 8, RANK), 1)
        inner = (lane >= k0) & (lane < k0 + 8)
        cols = [
            jnp.broadcast_to(jnp.sum(jnp.where(lane == k0 + j, first, 0.0), axis=2, keepdims=True), first.shape)
            for j in range(8)
        ]
        panel = jnp.where(inner, jnp.where(lane - k0 == sub, 1.0, 0.0), first)
        for j in range(0, 8, 2):
            one, two = cols[j], cols[j + 1]
            p, q = one[:, j : j + 1, :], two[:, j : j + 1, :]
            r, t = one[:, j + 1 : j + 2, :], two[:, j + 1 : j + 2, :]
            inv = 1.0 / (p * t - q * r)
            p, q, r, t = p * inv, q * inv, r * inv, t * inv

            def reduce_rows(x):
                u, v = x[:, j : j + 1, :], x[:, j + 1 : j + 2, :]
                y, z = t * u - q * v, p * v - r * u
                return jnp.where(sub == j, y, jnp.where(sub == j + 1, z, x - one * y - two * z))

            panel = reduce_rows(panel)
            cols = [reduce_rows(x) if i > j + 1 else x for i, x in enumerate(cols)]
        signed = jnp.where(lane < k0, -first, first)
        keep = (iota((RANK, RANK), 1) < k0) | (iota((RANK, RANK), 1) >= k0 + 8)
        for f in range(FOLDS):
            a1, a2, a3 = pieces(signed[f])
            b1, b2, b3 = pieces(panel[f])
            lhs = jnp.concatenate([a1, a1, a2, a2, a1, a3, jnp.zeros((80, RANK), jnp.float32)], axis=0).T
            rhs = jnp.concatenate([b1, b2, b1, b2, b3, b1, jnp.zeros((80, RANK), jnp.float32)], axis=0)
            change = dot(lhs.astype(jnp.bfloat16), rhs.astype(jnp.bfloat16))
            gram[f] = jnp.where(keep, gram[f], 0.0) - change
        gram[:, pl.ds(k0, 8), :] = panel

        f = lax.rem(b, FOLDS)
        q = pl.multiple_of(b // FOLDS * quarter, quarter)
        part_cols = pl.ds(q, quarter)
        sort = kind[:, part_cols]
        left_f = lw[:, pl.ds(pl.multiple_of(f * RANK, RANK), RANK)]
        guess = dot(left_f, right[f, part_cols, :], NT).astype(jnp.bfloat16)
        train = (sort > 0.5) & (sort != (f + 1).astype(jnp.bfloat16))
        missing = jnp.where(train, jnp.zeros_like(guess), guess)
        cross[f, :, part_cols] = dot(lt[f], missing)
        ahead = lax.rem(b // FOLDS + 1, FOLDS)
        classify(pl.multiple_of(f * tall, tall), pl.multiple_of(ahead * quarter, quarter))
        return carry

    def collect(at):
        swap_recv(*datas[at])
        cols = slice(at * part, (at + 1) * part)

        arrived = got[:, :, cols].reshape(CORE, part)
        present = kind[0:CORE, cols].astype(jnp.float32) > 0.5
        dw[0:CORE, cols] = jnp.where(present, dot(umat[...], arrived), 0.0).astype(jnp.bfloat16)
        dpack[:, cols] = dot(pick, dw[0:CORE, cols]).astype(jnp.bfloat16)
        halo_start(*halos[at])

    def finish(at):
        cols = slice(at * part, (at + 1) * part)
        halo_recv(*halos[at])
        known = dot(ltm[...], dw[:, cols])
        newb = []
        for f in range(FOLDS):
            total = known[f * RANK : (f + 1) * RANK, :] + cross[f, :, cols]
            a1, a2, a3 = pieces(gram[f])
            b1, b2, b3 = pieces(total)
            lhs = jnp.concatenate([a1, a1, a2, a2, a1, a3], axis=1).astype(jnp.bfloat16)
            rhs = jnp.concatenate([b1, b2, b1, b2, b3, b1], axis=0).astype(jnp.bfloat16)
            update = dot(lhs, rhs)
            cross[f, :, cols] = update
            newb.append(update.astype(jnp.bfloat16))
        chosen = dot(csel[...], jnp.concatenate(newb, axis=0))
        live = kind[0:CORE, cols].astype(jnp.float32) > 0.5
        diff = dw[0:CORE, cols].astype(jnp.float32) - chosen
        resid = jnp.where(live, diff, 0.0).astype(jnp.bfloat16)
        block = dot(vmat[...], resid).astype(jnp.bfloat16)
        back[:, :, cols] = block.reshape(peers, cap, part)
        ret[me, :, cols] = back[me, :, cols]
        swap_start(*rets[at])

    def deliver(at):
        cols = slice(at * part, (at + 1) * part)
        swap_recv(*rets[at])
        out[:, cols] = dot(qmat[...], ret[:, :, cols].reshape(CORE, part)).astype(jnp.bfloat16)

    lax.fori_loop(0, steps // 2, eliminate, 0)
    collect(0)
    lax.fori_loop(steps // 2, steps, eliminate, 0)
    collect(1)
    for at in range(PARTS):
        finish(at)
        if at + 2 < PARTS:
            collect(at + 2)

    for f in range(FOLDS):
        news[f] = cross[f].T

    for at in range(PARTS):
        deliver(at)

    swap_sent(*metas)
    halo_sent(*lefts)
    halo_sent(*folds)
    for at in range(PARTS):
        swap_sent(*datas[at])
        swap_sent(*rets[at])
        halo_sent(*halos[at])


def fused(acq_traces, route_owner, route_row, route_fold, sample_bits, left_factors, right_factors):
    n_long = lax.axis_size("mlong")
    n_short = lax.axis_size("mshort")
    peers = n_long * n_short
    rows, width = acq_traces.shape
    cap = rows // peers
    low = jnp.bitwise_and(sample_bits, 255).astype(jnp.bfloat16)
    high = lax.shift_right_logical(sample_bits, 8).astype(jnp.bfloat16)
    side = jnp.concatenate([left_factors.reshape(rows, WIDE), low, high], axis=1)
    vmem = pl.BlockSpec(memory_space=pltpu.VMEM)
    bf = jnp.bfloat16
    dma = pltpu.SemaphoreType.DMA
    return pl.pallas_call(
        functools.partial(kernel, n_long, n_short),
        out_shape=(
            jax.ShapeDtypeStruct((FOLDS, width, RANK), jnp.float32),
            jax.ShapeDtypeStruct((rows, width), bf),
        ),
        in_specs=[vmem] * 6,
        out_specs=(vmem, vmem),
        scratch_shapes=[
            pltpu.VMEM((WIN, WIDE + 128), bf),
            pltpu.VMEM((PACK, WIDE + 128), bf),
            pltpu.VMEM((WIN, 128), bf),
            pltpu.VMEM((PACK, 128), bf),
            pltpu.VMEM((WIN, width), bf),
            pltpu.VMEM((PACK, width), bf),
            pltpu.VMEM((peers, 1, 128), jnp.float32),
            pltpu.VMEM((peers, 1, 128), jnp.float32),
            pltpu.VMEM((peers, cap, width), bf),
            pltpu.VMEM((peers, cap, width), bf),
            pltpu.VMEM((peers, cap, width), bf),
            pltpu.VMEM((peers, cap, width), bf),
            pltpu.VMEM((WIN, width), bf),
            pltpu.VMEM((FOLDS, RANK, width), jnp.float32),
            pltpu.VMEM((FOLDS, RANK, WIN), bf),
            pltpu.VMEM((WIDE, WIN), bf),
            pltpu.VMEM((FOLDS, RANK, RANK), jnp.float32),
            pltpu.VMEM((CORE, CORE), bf),
            pltpu.VMEM((CORE, CORE), bf),
            pltpu.VMEM((CORE, CORE), bf),
            pltpu.VMEM((CORE, WIDE), bf),
            pltpu.VMEM((128, width), bf),
            dma((1,)), dma((1,)), dma((PARTS,)), dma((PARTS,)), dma((PARTS,)), dma((PARTS,)),
            dma((1, 8)), dma((1, 8)), dma((1, 8)), dma((1, 8)), dma((PARTS, 8)), dma((PARTS, 8)),
        ],
        compiler_params=pltpu.CompilerParams(
            collective_id=0, has_side_effects=True, vmem_limit_bytes=40 * 1024 * 1024
        ),
    )(
        acq_traces, route_owner.reshape(1, rows), route_row.reshape(1, rows), route_fold.reshape(1, rows),
        side, right_factors,
    )


def solution(mesh):
    in_specs = (
        P(("mlong", "mshort"), None),
        P(("mlong", "mshort")),
        P(("mlong", "mshort")),
        P(("mlong", "mshort")),
        P(("mlong", "mshort"), None),
        P(("mlong", "mshort"), None, None),
        P(None, ("mlong", "mshort"), None),
    )
    out_specs = (P(None, ("mlong", "mshort"), None), P(("mlong", "mshort"), None))
    peers = mesh.shape["mlong"] * mesh.shape["mshort"]
    body = fused if peers * 16 == CX * CY else local
    return jax.shard_map(body, mesh=mesh, in_specs=in_specs, out_specs=out_specs, check_vma=False)
```

```python
import functools

import jax
import jax.numpy as jnp
from jax import lax
from jax.experimental import pallas as pl
from jax.experimental.pallas import tpu as pltpu
from jax.sharding import PartitionSpec as P

RANK = 128
FOLDS = 4
H = 4
CX = 16
CY = 32


def padded(x, sides, width):
    for axis, dim in sides:
        count, length = (lax.axis_size(axis), x.shape[dim])
        up = [(i, (i + 1) % count) for i in range(count - 1)]
        down = [(j, i) for i, j in up]
        last = lax.slice_in_dim(x, length - width, length, axis=dim)
        initial = lax.slice_in_dim(x, 0, width, axis=dim)
        before = lax.ppermute(last, axis, up)
        after = lax.ppermute(initial, axis, down)
        x = jnp.concatenate([before, x, after], axis=dim)
    return x


def unpack(bits):
    shifts = jnp.arange(16, dtype=jnp.int32)
    flags = jnp.bitwise_and(lax.shift_right_logical(bits[:, :, None], shifts[None, None, :]), 1)
    return flags.reshape(bits.shape[0], -1).astype(jnp.float32)


def chol_right(cross, gram):
    chol = jnp.linalg.cholesky(gram)
    first = lax.linalg.triangular_solve(chol, cross, left_side=False, lower=True, transpose_a=True)
    return lax.linalg.triangular_solve(chol, first, left_side=False, lower=True, transpose_a=False)


def local(acq_traces, route_owner, route_row, route_fold, sample_bits, left_factors, right_factors):
    n_long = lax.axis_size("mlong")
    n_short = lax.axis_size("mshort")
    peers = n_long * n_short
    rows = acq_traces.shape[0]
    width = acq_traces.shape[1]
    cap = rows // peers
    total = peers * cap
    grid_bits = sample_bits.reshape(CX, CY, width // 16)
    grid_left = left_factors.reshape(CX, CY, FOLDS * RANK)
    valid = route_owner >= 0
    owner = jnp.where(valid, route_owner, 0)
    onehot = (
        (owner[:, None] == jnp.arange(peers, dtype=jnp.int32)[None, :]) & valid[:, None]
    ).astype(jnp.int32)
    within = jnp.sum(jnp.cumsum(onehot, axis=0) * onehot, axis=1) - 1
    place = jnp.where(valid, owner * cap + within, total)
    source = (
        jnp.full((total,), rows, jnp.int32)
        .at[place]
        .set(jnp.arange(rows, dtype=jnp.int32), mode="drop")
    )
    filled_slot = source < rows
    pick = jnp.minimum(source, rows - 1)
    send_traces = jnp.where(
        filled_slot[:, None], jnp.take(acq_traces, pick, axis=0), jnp.zeros((), jnp.bfloat16)
    )
    send_rows = jnp.where(filled_slot, jnp.take(route_row, pick), -1)
    send_folds = jnp.where(filled_slot, jnp.take(route_fold, pick), -1)
    got_traces, got_rows, got_folds = (
        lax.all_to_all(send_traces, ("mlong", "mshort"), split_axis=0, concat_axis=0, tiled=True),
        lax.all_to_all(send_rows, ("mlong", "mshort"), split_axis=0, concat_axis=0, tiled=True),
        lax.all_to_all(send_folds, ("mlong", "mshort"), split_axis=0, concat_axis=0, tiled=True),
    )
    arrival = (
        jnp.full((rows,), total, jnp.int32)
        .at[jnp.where(got_rows >= 0, got_rows, rows)]
        .set(jnp.arange(total, dtype=jnp.int32), mode="drop")
    )
    present = arrival < total
    slot_at = jnp.minimum(arrival, total - 1)
    data = jnp.where(
        present[:, None], jnp.take(got_traces, slot_at, axis=0), jnp.zeros((), jnp.bfloat16)
    )
    fold = jnp.where(present, jnp.take(got_folds, slot_at), -1)
    wide_data, wide_bits, wide_fold, wide_left = (
        padded(data.reshape(CX, CY, width), (("mlong", 0), ("mshort", 1)), H),
        padded(grid_bits, (("mlong", 0), ("mshort", 1)), H),
        padded(fold.reshape(CX, CY), (("mlong", 0), ("mshort", 1)), H),
        padded(grid_left, (("mlong", 0), ("mshort", 1)), H),
    )
    d_win = wide_data.reshape(-1, width)
    f_win = wide_fold.reshape(-1)
    l_win = wide_left.reshape(-1, FOLDS, RANK)
    seen = unpack(wide_bits.reshape(-1, width // 16)) * (f_win >= 0)[:, None].astype(jnp.float32)
    s_core = unpack(sample_bits) * (fold >= 0)[:, None].astype(jnp.float32)
    ridge = jnp.eye(RANK, dtype=jnp.float32)
    updates = []
    chosen = jnp.zeros((rows, width), jnp.float32)
    for f in range(FOLDS):
        factor = l_win[:, f]
        pred = jnp.dot(factor, right_factors[f].T, preferred_element_type=jnp.float32)
        train = seen * (f_win != f)[:, None].astype(jnp.float32)
        imputed = (train * d_win.astype(jnp.float32) + (1.0 - train) * pred).astype(jnp.bfloat16)
        cross = jnp.dot(imputed.T, factor, preferred_element_type=jnp.float32)
        gram = jnp.dot(factor.T, factor, preferred_element_type=jnp.float32) + ridge
        update = chol_right(cross, gram)
        updates.append(update)
        core_pred = jnp.dot(
            left_factors[:, f], update.astype(jnp.bfloat16).T, preferred_element_type=jnp.float32
        )
        chosen = chosen + (fold == f)[:, None].astype(jnp.float32) * core_pred
    new_right = jnp.stack(updates)
    resid = (s_core * (data.astype(jnp.float32) - chosen)).astype(jnp.bfloat16)
    back = jnp.where(
        (got_rows >= 0)[:, None],
        jnp.take(resid, jnp.maximum(got_rows, 0), axis=0),
        jnp.zeros((), jnp.bfloat16),
    )
    returned = lax.all_to_all(back, ("mlong", "mshort"), split_axis=0, concat_axis=0, tiled=True)
    trace_residuals = jnp.where(
        valid[:, None],
        jnp.take(returned, jnp.minimum(place, total - 1), axis=0),
        jnp.zeros((), jnp.bfloat16),
    )
    return (new_right, trace_residuals)


MESH = pl.DeviceIdType.MESH
WIN = 1024
CORE = CX * CY
WIDE = FOLDS * RANK
PARTS = 2
NT = (((1,), (1,)), ((), ()))
HALO = (
    (1, 0, False, CORE - H * CY, CORE, H * CY),
    (-1, 0, False, 0, CORE + H * CY, H * CY),
    (0, 1, True, H * CX, CORE + 2 * H * CY, H * CX),
    (0, -1, True, 0, CORE + 2 * H * CY + H * CX, H * CX),
    (1, 1, True, 2 * H * CX + 48, CORE + 2 * H * (CX + CY), 16),
    (1, -1, True, 2 * H * CX + 32, CORE + 2 * H * (CX + CY) + 16, 16),
    (-1, 1, True, 2 * H * CX + 16, CORE + 2 * H * (CX + CY) + 32, 16),
    (-1, -1, True, 2 * H * CX, CORE + 2 * H * (CX + CY) + 48, 16),
)
PACK = 2 * H * CX + 64


def iota(shape, dim):
    return lax.broadcasted_iota(jnp.int32, shape, dim)


def flags(mask, dtype=jnp.bfloat16):
    return jnp.where(mask, 1.0, 0.0).astype(dtype)


def dot(a, b, dims=(((1,), (0,)), ((), ())), precision=None):
    return lax.dot_general(a, b, dims, precision=precision, preferred_element_type=jnp.float32)


def div(x, n):
    return lax.shift_right_arithmetic(x, n.bit_length() - 1)


def mod(x, n):
    return x & (n - 1)


def packed_rows(shape):
    t = iota(shape, 0)
    u = t - 2 * H * CX
    v = mod(t, H * CX)
    edge = div(v, H) * CY + mod(v, H) + jnp.where(t < H * CX, 0, CY - H)
    k = div(u, 16)
    w = mod(u, 16)
    corner = (div(w, H) + jnp.where(k >= 2, CX - H, 0)) * CY + mod(w, H) + jnp.where(mod(k, 2) == 1, CY - H, 0)
    return jnp.where(u < 0, edge, corner)


def pieces(x):
    top = x.astype(jnp.bfloat16).astype(jnp.float32)
    rest = x - top
    middle = rest.astype(jnp.bfloat16).astype(jnp.float32)
    return top, middle, rest - middle


def kernel(
    n_long, n_short, traces, own, row, fold, side, right, news, out,
    lw, lpack, fw, fpack, dw, dpack, meta_out, meta_in, send, got, ret, back, pred, kind, cross, lt, gram, umat, vmat, qmat, csel,
    meta_s, meta_r, data_s, data_r, ret_s, ret_r, hl_s, hl_r, hf_s, hf_r, hd_s, hd_r,
):
    peers = n_long * n_short
    cap = CORE // peers
    a = lax.axis_index("mlong")
    c = lax.axis_index("mshort")
    me = a * n_short + c
    width = traces.shape[1]

    lw[0:CORE, :] = side[...]
    lw[CORE:WIN, :] = jnp.zeros((WIN - CORE, WIDE + 128), jnp.bfloat16)
    fw[CORE:WIN, :] = jnp.zeros((WIN - CORE, 128), jnp.bfloat16)
    dw[CORE:WIN, :] = jnp.zeros((WIN - CORE, width), jnp.bfloat16)
    part = width // PARTS

    barrier = pltpu.get_barrier_semaphore()

    others = [None]
    for k in range(1, peers):
        q = lax.rem(me + k, peers)
        others.append((q, (q // n_short, lax.rem(q, n_short))))
        pl.semaphore_signal(barrier, inc=1, device_id=others[k][1], device_id_type=MESH)

    owner = own[...]
    oh = flags(iota((peers, CORE), 0) == owner, jnp.float32)
    tri = flags(iota((CORE, CORE), 0) < iota((CORE, CORE), 1))
    cum = dot(oh.astype(jnp.bfloat16), tri)
    within = jnp.sum(oh * cum, axis=0, keepdims=True).astype(jnp.int32)
    place = jnp.where(owner >= 0, owner * cap + within, -1)
    rows = row[...]
    vals = [div(rows, 128).astype(jnp.float32), mod(rows, 128).astype(jnp.float32), (fold[...] + 1).astype(jnp.float32)]
    left = jnp.concatenate([oh * v for v in vals], axis=1).astype(jnp.bfloat16)
    rightm = jnp.concatenate([flags(iota((128, CORE), 0) == within + 32 * i) for i in range(3)], axis=1)
    meta = dot(left, rightm, NT)
    for p in range(peers):
        meta_out[p] = meta[p : p + 1, :]
    meta_in[me] = meta_out[me]

    pl.semaphore_wait(barrier, peers - 1)

    def halo(buffer, pack, send_sem, recv_sem, at, span, i):
        da, dc, packed, start, dst, count = HALO[i]
        here = pack if packed else buffer
        return pltpu.make_async_remote_copy(
            src_ref=here.at[pl.ds(start, count), pl.ds(at * span, span)],
            dst_ref=buffer.at[pl.ds(dst, count), pl.ds(at * span, span)],
            send_sem=send_sem.at[at, i],
            recv_sem=recv_sem.at[at, i],
            device_id=(a + da, c + dc),
            device_id_type=MESH,
        )

    def inside(da, dc):
        return (a + da >= 0) & (a + da < n_long) & (c + dc >= 0) & (c + dc < n_short)

    def halo_start(*refs):
        for i in range(8):
            @pl.when(inside(HALO[i][0], HALO[i][1]))
            def _():
                halo(*refs, i).start()

    def halo_recv(*refs):
        for i in range(8):
            @pl.when(inside(-HALO[i][0], -HALO[i][1]))
            def _():
                halo(*refs, i).wait_recv()

    def halo_sent(*refs):
        for i in range(8):
            @pl.when(inside(HALO[i][0], HALO[i][1]))
            def _():
                halo(*refs, i).wait_send()

    def swap(src, dst, send_sem, recv_sem, at, span, k):
        to, place_of_to = others[k]
        return pltpu.make_async_remote_copy(
            src_ref=src.at[to, :, pl.ds(at * span, span)],
            dst_ref=dst.at[me, :, pl.ds(at * span, span)],
            send_sem=send_sem.at[at],
            recv_sem=recv_sem.at[at],
            device_id=place_of_to,
            device_id_type=MESH,
        )

    def all_of(src, dst, send_sem, recv_sem, at, span):
        return pltpu.make_async_remote_copy(
            src_ref=src.at[pl.ds(1, peers - 1), :, pl.ds(at * span, span)],
            dst_ref=dst.at[pl.ds(1, peers - 1), :, pl.ds(at * span, span)],
            send_sem=send_sem.at[at],
            recv_sem=recv_sem.at[at],
            device_id=(a, lax.rem(c + 1, n_short)),
            device_id_type=MESH,
        )

    def swap_start(*refs):
        for k in range(1, peers):
            swap(*refs, k).start()

    def swap_recv(*refs):
        all_of(*refs).wait_recv()

    def swap_sent(*refs):
        all_of(*refs).wait_send()

    metas = (meta_out, meta_in, meta_s, meta_r, 0, 128)
    datas = [(send, got, data_s, data_r, at, part) for at in range(PARTS)]
    rets = [(back, ret, ret_s, ret_r, at, part) for at in range(PARTS)]
    lefts = (lw, lpack, hl_s, hl_r, 0, WIDE + 128)
    folds = (fw, fpack, hf_s, hf_r, 0, 128)
    halos = [(dw, dpack, hd_s, hd_r, at, part) for at in range(PARTS)]
    swap_start(*metas)

    take = flags(iota((CORE, CORE), 0) == place)
    for at in range(PARTS):
        cols = slice(at * part, (at + 1) * part)
        send[:, :, cols] = dot(take, traces[:, cols]).astype(jnp.bfloat16).reshape(peers, cap, part)
        swap_start(*datas[at])
    got[me] = send[me]

    pick = flags(packed_rows((PACK, CORE)) == iota((PACK, CORE), 1))
    lpack[...] = dot(pick, side[...]).astype(jnp.bfloat16)
    halo_start(*lefts)

    eye = iota((CORE, CORE), 0) == iota((CORE, CORE), 1)

    def column(line):
        return jnp.sum(jnp.where(eye, line.astype(jnp.float32), 0.0), axis=1, keepdims=True).astype(jnp.int32)

    qmat[...] = flags(column(place) == iota((CORE, CORE), 1))

    swap_recv(*metas)
    meta_got = meta_in[:, 0, :].astype(jnp.bfloat16)
    mine = iota((peers, CORE), 0) == div(iota((peers, CORE), 1), cap)
    lines = []
    for i in range(3):
        place_of = flags(iota((128, CORE), 0) == mod(iota((128, CORE), 1), cap) + 32 * i)
        lines.append(jnp.sum(jnp.where(mine, dot(meta_got, place_of), 0.0), axis=0, keepdims=True))
    got_row = jnp.where(lines[2] > 0.5, lines[0] * 128.0 + lines[1], -1.0).astype(jnp.int32)
    got_fold = jnp.broadcast_to(lines[2], (128, CORE)).astype(jnp.bfloat16)
    umat[0:CORE, :] = flags(iota((CORE, CORE), 0) == got_row)
    umat[CORE : CORE + PACK, :] = flags(packed_rows((PACK, CORE)) == got_row)
    fw[0:CORE, :] = dot(umat[0:CORE, :], got_fold, NT).astype(jnp.bfloat16)
    fpack[...] = dot(umat[CORE : CORE + PACK, :], got_fold, NT).astype(jnp.bfloat16)
    halo_start(*folds)
    vmat[...] = flags(column(got_row) == iota((CORE, CORE), 1))
    for f in range(FOLDS):
        fs = slice(f * RANK, (f + 1) * RANK)
        csel[:, fs] = jnp.where(fw[0:CORE, :] == f + 1.0, side[:, fs], jnp.zeros((CORE, RANK), jnp.bfloat16))

    halo_recv(*lefts)
    for f in range(FOLDS):
        factor = lw[:, f * RANK : (f + 1) * RANK]
        lt[f] = factor.T
        ident = flags(iota((RANK, RANK), 0) == iota((RANK, RANK), 1), jnp.float32)
        gram[f] = dot(lt[f], factor) + ident

    halo_recv(*folds)
    words = iota((128, width), 0)
    offs = iota((128, width), 1)
    expand = flags(words == div(offs, 16) + jnp.where(mod(offs, 16) >= 8, 64, 0))
    steps = RANK // 8
    tall = WIN // steps
    quarter = FOLDS * width // steps

    def eliminate(b, carry):
        k0 = pl.multiple_of(b * 8, 8)
        first = gram[:, pl.ds(k0, 8), :]
        lane = iota((FOLDS, 8, RANK), 2)
        sub = iota((FOLDS, 8, RANK), 1)
        inner = (lane >= k0) & (lane < k0 + 8)
        cols = [
            jnp.broadcast_to(jnp.sum(jnp.where(lane == k0 + j, first, 0.0), axis=2, keepdims=True), first.shape)
            for j in range(8)
        ]
        panel = jnp.where(inner, jnp.where(lane - k0 == sub, 1.0, 0.0), first)
        for j in range(0, 8, 2):
            one, two = cols[j], cols[j + 1]
            p, q = one[:, j : j + 1, :], two[:, j : j + 1, :]
            r, t = one[:, j + 1 : j + 2, :], two[:, j + 1 : j + 2, :]
            inv = 1.0 / (p * t - q * r)
            p, q, r, t = p * inv, q * inv, r * inv, t * inv

            def reduce_rows(x):
                u, v = x[:, j : j + 1, :], x[:, j + 1 : j + 2, :]
                y, z = t * u - q * v, p * v - r * u
                return jnp.where(sub == j, y, jnp.where(sub == j + 1, z, x - one * y - two * z))

            panel = reduce_rows(panel)
            cols = [reduce_rows(x) if i > j + 1 else x for i, x in enumerate(cols)]
        signed = jnp.where(lane < k0, -first, first)
        keep = (iota((RANK, RANK), 1) < k0) | (iota((RANK, RANK), 1) >= k0 + 8)
        for f in range(FOLDS):
            a1, a2, a3 = pieces(signed[f])
            b1, b2, b3 = pieces(panel[f])
            lhs = jnp.concatenate([a1, a1, a2, a2, a1, a3, jnp.zeros((80, RANK), jnp.float32)], axis=0).T
            rhs = jnp.concatenate([b1, b2, b1, b2, b3, b1, jnp.zeros((80, RANK), jnp.float32)], axis=0)
            change = dot(lhs.astype(jnp.bfloat16), rhs.astype(jnp.bfloat16))
            gram[f] = jnp.where(keep, gram[f], 0.0) - change
        gram[:, pl.ds(k0, 8), :] = panel

        r = pl.ds(pl.multiple_of(b * tall, tall), tall)
        byte = dot(lw[r, WIDE : WIDE + 128], expand).astype(jnp.int32)
        bit = lax.shift_right_logical(byte, mod(iota((tall, width), 1), 8)) & 1
        flag = bit.astype(jnp.float32).astype(jnp.bfloat16)
        kind[r, :] = jnp.concatenate([fw[r, :]] * (width // 128), axis=1) * flag

        f = b // (steps // FOLDS)
        q = pl.ds(pl.multiple_of(lax.rem(b, steps // FOLDS) * quarter, quarter), quarter)
        left_f = lw[:, pl.ds(pl.multiple_of(f * RANK, RANK), RANK)]
        pred[f, :, q] = dot(left_f, right[f, q, :], NT).astype(jnp.bfloat16)
        return carry

    def collect(at):
        swap_recv(*datas[at])
        cols = slice(at * part, (at + 1) * part)

        arrived = got[:, :, cols].reshape(CORE, part)
        dpack[:, cols] = dot(umat[CORE : CORE + PACK, :], arrived).astype(jnp.bfloat16)
        dw[0:CORE, cols] = dot(umat[0:CORE, :], arrived).astype(jnp.bfloat16)
        halo_start(*halos[at])

    def finish(at):
        cols = slice(at * part, (at + 1) * part)
        halo_recv(*halos[at])
        newb = []
        for f in range(FOLDS):
            sort = kind[:, cols]
            train = (sort > 0.5) & (sort != f + 1.0)
            filled = jnp.where(train, dw[:, cols], pred[f, :, cols])
            total = dot(lt[f], filled)
            update = dot(gram[f], total, precision=lax.Precision.HIGHEST)
            cross[f, :, cols] = update
            newb.append(update.astype(jnp.bfloat16))
        chosen = dot(csel[...], jnp.concatenate(newb, axis=0))
        live = kind[0:CORE, cols].astype(jnp.float32) > 0.5
        diff = dw[0:CORE, cols].astype(jnp.float32) - chosen
        resid = jnp.where(live, diff, 0.0).astype(jnp.bfloat16)
        block = dot(vmat[...], resid).astype(jnp.bfloat16)
        back[:, :, cols] = block.reshape(peers, cap, part)
        ret[me, :, cols] = back[me, :, cols]
        swap_start(*rets[at])

    def deliver(at):
        cols = slice(at * part, (at + 1) * part)
        swap_recv(*rets[at])
        out[:, cols] = dot(qmat[...], ret[:, :, cols].reshape(CORE, part)).astype(jnp.bfloat16)

    lax.fori_loop(0, steps, eliminate, 0)
    collect(0)
    collect(1)
    for at in range(PARTS):
        finish(at)
        if at + 2 < PARTS:
            collect(at + 2)

    for f in range(FOLDS):
        news[f] = cross[f].T

    for at in range(PARTS):
        deliver(at)

    swap_sent(*metas)
    halo_sent(*lefts)
    halo_sent(*folds)
    for at in range(PARTS):
        swap_sent(*datas[at])
        swap_sent(*rets[at])
        halo_sent(*halos[at])


def fused(acq_traces, route_owner, route_row, route_fold, sample_bits, left_factors, right_factors):
    n_long = lax.axis_size("mlong")
    n_short = lax.axis_size("mshort")
    peers = n_long * n_short
    rows, width = acq_traces.shape
    cap = rows // peers
    low = jnp.bitwise_and(sample_bits, 255).astype(jnp.bfloat16)
    high = lax.shift_right_logical(sample_bits, 8).astype(jnp.bfloat16)
    side = jnp.concatenate([left_factors.reshape(rows, WIDE), low, high], axis=1)
    vmem = pl.BlockSpec(memory_space=pltpu.VMEM)
    bf = jnp.bfloat16
    dma = pltpu.SemaphoreType.DMA
    return pl.pallas_call(
        functools.partial(kernel, n_long, n_short),
        out_shape=(
            jax.ShapeDtypeStruct((FOLDS, width, RANK), jnp.float32),
            jax.ShapeDtypeStruct((rows, width), bf),
        ),
        in_specs=[vmem] * 6,
        out_specs=(vmem, vmem),
        scratch_shapes=[
            pltpu.VMEM((WIN, WIDE + 128), bf),
            pltpu.VMEM((PACK, WIDE + 128), bf),
            pltpu.VMEM((WIN, 128), bf),
            pltpu.VMEM((PACK, 128), bf),
            pltpu.VMEM((WIN, width), bf),
            pltpu.VMEM((PACK, width), bf),
            pltpu.VMEM((peers, 1, 128), jnp.float32),
            pltpu.VMEM((peers, 1, 128), jnp.float32),
            pltpu.VMEM((peers, cap, width), bf),
            pltpu.VMEM((peers, cap, width), bf),
            pltpu.VMEM((peers, cap, width), bf),
            pltpu.VMEM((peers, cap, width), bf),
            pltpu.VMEM((FOLDS, WIN, width), bf),
            pltpu.VMEM((WIN, width), bf),
            pltpu.VMEM((FOLDS, RANK, width), jnp.float32),
            pltpu.VMEM((FOLDS, RANK, WIN), bf),
            pltpu.VMEM((FOLDS, RANK, RANK), jnp.float32),
            pltpu.VMEM((CORE + PACK, CORE), bf),
            pltpu.VMEM((CORE, CORE), bf),
            pltpu.VMEM((CORE, CORE), bf),
            pltpu.VMEM((CORE, WIDE), bf),
            dma((1,)), dma((1,)), dma((PARTS,)), dma((PARTS,)), dma((PARTS,)), dma((PARTS,)),
            dma((1, 8)), dma((1, 8)), dma((1, 8)), dma((1, 8)), dma((PARTS, 8)), dma((PARTS, 8)),
        ],
        compiler_params=pltpu.CompilerParams(
            collective_id=0, has_side_effects=True, vmem_limit_bytes=44 * 1024 * 1024
        ),
    )(
        acq_traces, route_owner.reshape(1, rows), route_row.reshape(1, rows), route_fold.reshape(1, rows),
        side, right_factors,
    )


def solution(mesh):
    in_specs = (
        P(("mlong", "mshort"), None),
        P(("mlong", "mshort")),
        P(("mlong", "mshort")),
        P(("mlong", "mshort")),
        P(("mlong", "mshort"), None),
        P(("mlong", "mshort"), None, None),
        P(None, ("mlong", "mshort"), None),
    )
    out_specs = (P(None, ("mlong", "mshort"), None), P(("mlong", "mshort"), None))
    peers = mesh.shape["mlong"] * mesh.shape["mshort"]
    body = fused if peers * 16 == CX * CY else local
    return jax.shard_map(body, mesh=mesh, in_specs=in_specs, out_specs=out_specs, check_vma=False)
```
